256 devices in a mesh: quad: 8 (over x, z_hi), py: 8 (over y, core), pz: 4 (over z_lo).
Axes of the slice: x: 4, y: 4, z: 8 (z_hi: 2, z_lo: 4; z = z_hi * 4 + z_lo), core: 2. Of those that a mesh axis runs over, the one named last changes fastest.
Arguments:
- source_real: float32 [4, 16, 128, 512], P(None, None, 'py', 'pz'), may hold values from -6 to 6
- source_imag: float32 [4, 16, 128, 512], P(None, None, 'py', 'pz'), may hold values from -2 to 2
- potential: float32 [16, 128, 512], P(None, 'py', 'pz'), may hold values from 0 to 2
- center: float32 [1], replicated, may hold values from 4.5 to 6
- radius: float32 [1], replicated, may hold values from 1 to 2
Outputs:
- moments: float32 [4, 2, 4, 16, 128, 512], P(None, None, None, 'quad', 'py', 'pz')
The draws below stay inside these ranges and needn't reach their ends.
All inputs are finite; a program needn't handle non-finite values.
Results may differ from the reference program's by a relative error of at most 0.0003.
Values sent between devices are 32-bit elements; how exact they have to be, the bound alone decides.
A program may use at most 128 MiB of HBM per device.

```python
import math
import jax
import jax.numpy as jnp

CX = 16
SRC = 4
QPTS = 8
MOMS = 4
NY = 128
NZ = 512


def levels(own_key, shape, pieces, least, largest):
    def one(axis_at, blocks):
        heights = jax.random.uniform(jax.random.fold_in(jax.random.fold_in(own_key, 6), axis_at), (blocks,), jnp.float32, least / len(pieces), largest / len(pieces))
        return jnp.repeat(jnp.exp(heights), shape[axis_at] // blocks).reshape((-1,) + (1,) * (len(shape) - axis_at - 1))

    level = one(*pieces[0])
    for cut in pieces[1:]:
        level = level * one(*cut)
    return level


def normal_values(stream_key, dims, width, most, cuts=(), kind=jnp.bfloat16):
    entries = jax.random.normal(stream_key, dims, jnp.float32) * width
    if len(cuts) > 0:
        entries = levels(stream_key, dims, cuts, -0.22, 0.18) * entries
    return jnp.clip(entries, min=-most, max=most).astype(kind)


def setup_inputs(seed: int = 0) -> dict:
    seeds = jax.random.split(jax.random.key(seed), 6)
    source_real = normal_values(seeds[0], (SRC, CX, NY, NZ), 1.0, 6.0, ((2, 8), (3, 4)), jnp.float32)
    source_imag = normal_values(seeds[1], (SRC, CX, NY, NZ), 0.3, 2.0, ((2, 8), (3, 4)), jnp.float32)
    potential = jnp.clip(2.0 * jax.random.uniform(seeds[2], (CX, NY, NZ), jnp.float32) ** levels(seeds[2], (CX, NY, NZ), ((1, 8), (2, 4)), -0.2, 0.2), 0.0, 2.0)
    center = jnp.clip(jax.random.uniform(seeds[3], (1,), jnp.float32, 4.5, 6.0), 4.5, 6.0)
    radius = jnp.clip(jax.random.uniform(seeds[4], (1,), jnp.float32, 1.0, 2.0), 1.0, 2.0)
    return dict(source_real=source_real, source_imag=source_imag, potential=potential, center=center, radius=radius)


stencil_weights = (-205.0 / 72.0, 8.0 / 5.0, -1.0 / 5.0, 8.0 / 315.0, -1.0 / 560.0)


def hamiltonian(field, potential):
    laplace = 3.0 * stencil_weights[0] * field
    for offset in range(1, 5):
        beside_all = jnp.roll(field, offset, -3) + jnp.roll(field, -offset, -3)
        beside_all = beside_all + jnp.roll(field, offset, -2) + jnp.roll(field, -offset, -2)
        beside_all = beside_all + jnp.roll(field, offset, -1) + jnp.roll(field, -offset, -1)
        laplace = laplace + stencil_weights[offset] * beside_all
    return -0.5 * laplace + potential * field


def complex_mul(left, right):
    return (left[0] * right[0] - left[1] * right[1], left[0] * right[1] + left[1] * right[0])


def complex_div(left, right):
    norm_sq = right[0] * right[0] + right[1] * right[1]
    return ((left[0] * right[0] + left[1] * right[1]) / norm_sq, (left[1] * right[0] - left[0] * right[1]) / norm_sq)


def bilinear(left, right):
    both = complex_mul(left, right)
    return (jnp.sum(both[0], axis=(-3, -2, -1)), jnp.sum(both[1], axis=(-3, -2, -1)))


def spread(value):
    return (value[0][..., None, None, None], value[1][..., None, None, None])


def reference(source_real, source_imag, potential, center, radius):
    source = (source_real, source_imag)
    applied = hamiltonian(jnp.stack(source), potential)
    hsource = (applied[0], applied[1])
    rho_first = bilinear(source, source)
    curv_first = bilinear(source, hsource)
    orders = jnp.arange(1, MOMS + 1).astype(jnp.float32)
    moment_re = jnp.zeros((MOMS,) + source_real.shape, jnp.float32)
    moment_im = jnp.zeros((MOMS,) + source_real.shape, jnp.float32)
    for point in range(QPTS):
        angle = 2.0 * math.pi * (point + 0.5) / QPTS
        shift = (center[0] + radius[0] * math.cos(angle), radius[0] * math.sin(angle))
        scaled = complex_mul(shift, rho_first)
        denom = (scaled[0] - curv_first[0], scaled[1] - curv_first[1])
        alpha_first = spread(complex_div(rho_first, denom))
        first_iterate = complex_mul(alpha_first, source)
        shifted = complex_mul(shift, source)
        image = (shifted[0] - hsource[0], shifted[1] - hsource[1])
        moved = complex_mul(alpha_first, image)
        residual = (source[0] - moved[0], source[1] - moved[1])
        rho_next = bilinear(residual, residual)
        beta = spread(complex_div(rho_next, rho_first))
        carried = complex_mul(beta, source)
        direction = (residual[0] + carried[0], residual[1] + carried[1])
        happ = hamiltonian(jnp.stack(direction), potential)
        shifted_dir = complex_mul(shift, direction)
        image_next = (shifted_dir[0] - happ[0], shifted_dir[1] - happ[1])
        alpha_next = spread(complex_div(rho_next, bilinear(direction, image_next)))
        step_part = complex_mul(alpha_next, direction)
        solution = (first_iterate[0] + step_part[0], first_iterate[1] + step_part[1])
        weight_re = (radius[0] / QPTS) * jnp.cos(orders * angle)
        weight_im = (radius[0] / QPTS) * jnp.sin(orders * angle)
        weight_re = weight_re[:, None, None, None, None]
        weight_im = weight_im[:, None, None, None, None]
        moment_re = moment_re + (weight_re * solution[0][None] - weight_im * solution[1][None])
        moment_im = moment_im + (weight_re * solution[1][None] + weight_im * solution[0][None])
    return jnp.stack([moment_re, moment_im], 1)
```

```python
import math

import jax
import jax.numpy as jnp
from jax import lax
from jax.sharding import PartitionSpec as P

QPTS = 8
MOMS = 4


stencil_weights = (-205.0 / 72.0, 8.0 / 5.0, -1.0 / 5.0, 8.0 / 315.0, -1.0 / 560.0)


def with_halo(value, sides, width):
    edges = {}
    for axis, dim in sides:
        count, length = (lax.axis_size(axis), value.shape[dim])
        up = [(i, (i + 1) % count) for i in range(count)]
        last = lax.slice_in_dim(value, length - width, length, axis=dim)
        initial = lax.slice_in_dim(value, 0, width, axis=dim)
        edges[dim] = (
            lax.ppermute(last, axis, up),
            lax.ppermute(initial, axis, [(b, a) for a, b in up]),
        )
    done = []
    for _, dim in sides:
        low, high = edges[dim]
        around = [(width, width) if d in done else (0, 0) for d in range(value.ndim)]
        value = jnp.concatenate([jnp.pad(low, around), value, jnp.pad(high, around)], axis=dim)
        done.append(dim)
    return value


def sent_to_all(value, axis):
    count = lax.axis_size(axis)
    return lax.all_to_all(
        jnp.broadcast_to(value[None], (count, *value.shape)), axis, 0, 0, tiled=True
    )


def over_copies(value, axis):
    return sent_to_all(value, axis).sum(axis=0)


def packed_total(arrays, axis):
    ends = [0]
    for a in arrays:
        ends.append(ends[-1] + a.size)
    running = over_copies(jnp.concatenate([a.ravel() for a in arrays]), axis)
    return tuple((running[b:e].reshape(a.shape) for a, b, e in zip(arrays, ends, ends[1:])))


def apply_operator(field, potential):
    padded = with_halo(field, (("py", 4), ("pz", 5)), 4)
    width_y = field.shape[4]
    width_z = field.shape[5]
    laplace = 3.0 * stencil_weights[0] * field
    for offset in range(1, 5):
        beside_all = jnp.roll(field, offset, 3) + jnp.roll(field, -offset, 3)
        beside_all = (
            beside_all + padded[:, :, :, :, 4 + offset : 4 + offset + width_y, 4 : 4 + width_z]
        )
        beside_all = (
            beside_all + padded[:, :, :, :, 4 - offset : 4 - offset + width_y, 4 : 4 + width_z]
        )
        beside_all = (
            beside_all + padded[:, :, :, :, 4 : 4 + width_y, 4 + offset : 4 + offset + width_z]
        )
        beside_all = (
            beside_all + padded[:, :, :, :, 4 : 4 + width_y, 4 - offset : 4 - offset + width_z]
        )
        laplace = laplace + stencil_weights[offset] * beside_all
    return -0.5 * laplace + potential * field


def complex_mul(left, right):
    return (left[0] * right[0] - left[1] * right[1], left[0] * right[1] + left[1] * right[0])


def complex_div(left, right):
    norm_sq = right[0] * right[0] + right[1] * right[1]
    return (
        (left[0] * right[0] + left[1] * right[1]) / norm_sq,
        (left[1] * right[0] - left[0] * right[1]) / norm_sq,
    )


def local_bilinear(left, right):
    both = complex_mul(left, right)
    return (jnp.sum(both[0], axis=(-3, -2, -1)), jnp.sum(both[1], axis=(-3, -2, -1)))


def spread(value):
    return (value[0][..., None, None, None], value[1][..., None, None, None])


def recip(value):
    return complex_div((jnp.ones_like(value[0]), jnp.zeros_like(value[0])), value)


def coefficients(totals, radius_value):
    mu0, mu1, mu2, mu3 = totals
    tau = complex_div(mu1, mu0)
    tau_mu1 = complex_mul(tau, mu1)
    nu2 = (mu2[0] - tau_mu1[0], mu2[1] - tau_mu1[1])
    tau_mu2 = complex_mul(tau, mu2)
    tau2_mu1 = complex_mul(tau, tau_mu1)
    nu3 = (mu3[0] - 2.0 * tau_mu2[0] + tau2_mu1[0], mu3[1] - 2.0 * tau_mu2[1] + tau2_mu1[1])
    ratio = complex_div(nu3, nu2)
    slope = complex_div(nu2, mu0)
    angles = 2.0 * math.pi * (jnp.arange(QPTS).astype(jnp.float32)[:, None] + 0.5) / QPTS
    shift = (radius_value * jnp.cos(angles), radius_value * jnp.sin(angles))
    alpha_first = recip((shift[0] - tau[0], shift[1] - tau[1]))
    gamma = complex_mul(alpha_first, slope)
    alpha_next = recip((shift[0] - ratio[0] - gamma[0], shift[1] - ratio[1] - gamma[1]))
    image_part = complex_mul(alpha_first, alpha_next)
    back = complex_mul(image_part, (gamma[0] - tau[0], gamma[1] - tau[1]))
    source_part = (alpha_first[0] + back[0], alpha_first[1] + back[1])
    orders = jnp.arange(1, MOMS + 1).astype(jnp.float32)
    phase = orders[:, None, None] * angles[None]
    weight = (radius_value / QPTS * jnp.cos(phase), radius_value / QPTS * jnp.sin(phase))
    out = []
    for part in (source_part, image_part):
        both = complex_mul(weight, (part[0][None], part[1][None]))
        out.append((jnp.sum(both[0], 1), jnp.sum(both[1], 1)))
    return out


def per_device(source_real, source_imag, potential, center, radius):
    source = jnp.stack((source_real, source_imag))
    shifted = potential - center[0]
    image = apply_operator(source[None], shifted)[0]
    image_two = apply_operator(image[None], shifted)[0]
    pairs = ((source, source), (source, image), (image, image), (image, image_two))
    parts = [local_bilinear((u[0], u[1]), (v[0], v[1])) for u, v in pairs]
    totals = packed_total([p for pair in parts for p in pair], ("py", "pz"))
    totals = [(totals[2 * i], totals[2 * i + 1]) for i in range(4)]
    source_weight, image_weight = coefficients(totals, radius[0])
    count = source_real.shape[1] // lax.axis_size("quad")
    first = lax.axis_index("quad") * count
    own = lax.dynamic_slice_in_dim(source, first, count, 2)
    own_image = lax.dynamic_slice_in_dim(image, first, count, 2)
    a = complex_mul(spread(source_weight), (own[0], own[1]))
    b = complex_mul(spread(image_weight), (own_image[0], own_image[1]))
    return jnp.stack([a[0] + b[0], a[1] + b[1]], 1)


def solution(mesh):
    in_specs = (P(None, None, "py", "pz"), P(None, None, "py", "pz"), P(None, "py", "pz"), P(), P())
    out_specs = P(None, None, None, "quad", "py", "pz")
    return jax.shard_map(
        per_device, mesh=mesh, in_specs=in_specs, out_specs=out_specs, check_vma=False
    )
```

```python
import functools
import math

import jax
import jax.numpy as jnp
import numpy as np
from jax import lax
from jax.experimental import pallas as pl
from jax.experimental.pallas import tpu as pltpu
from jax.sharding import PartitionSpec as P

QPTS = 8
MOMS = 4
MESH = pl.DeviceIdType.MESH
LANES = 128
REACH = 4
stencil_weights = (-205.0 / 72.0, 8.0 / 5.0, -1.0 / 5.0, 8.0 / 315.0, -1.0 / 560.0)
half_weights = tuple(-0.5 * w for w in stencil_weights)


def complex_mul(left, right):
    return (left[0] * right[0] - left[1] * right[1], left[0] * right[1] + left[1] * right[0])


def complex_div(left, right):
    norm_sq = right[0] * right[0] + right[1] * right[1]
    return (
        (left[0] * right[0] + left[1] * right[1]) / norm_sq,
        (left[1] * right[0] - left[0] * right[1]) / norm_sq,
    )


def complex_sub(left, right):
    return (left[0] - right[0], left[1] - right[1])


def recip(value):
    norm_sq = value[0] * value[0] + value[1] * value[1]
    return (value[0] / norm_sq, -value[1] / norm_sq)


def coefficients(totals, shift):
    mu0, mu1, mu2, mu3 = totals
    tau = complex_div(mu1, mu0)
    tau_mu1 = complex_mul(tau, mu1)
    nu2 = complex_sub(mu2, tau_mu1)
    tau_mu2 = complex_mul(tau, mu2)
    nu3 = complex_sub(complex_sub(mu3, tau_mu2), complex_mul(tau, complex_sub(mu2, tau_mu1)))
    ratio = complex_div(nu3, nu2)
    slope = complex_div(nu2, mu0)
    alpha_first = recip(complex_sub(shift, tau))
    gamma = complex_mul(alpha_first, slope)
    alpha_next = recip(complex_sub(complex_sub(shift, ratio), gamma))
    image_part = complex_mul(alpha_first, alpha_next)
    back = complex_mul(image_part, complex_sub(gamma, tau))
    return (alpha_first[0] + back[0], alpha_first[1] + back[1]), image_part


def tables():
    theta = 2.0 * math.pi * (np.arange(QPTS) + 0.5) / QPTS
    rows = [np.cos(theta), np.sin(theta)]
    for k in range(1, MOMS + 1):
        rows += [np.cos(k * theta) / QPTS, np.sin(k * theta) / QPTS]
    return np.broadcast_to(np.stack(rows)[:, :, None], (2 + 2 * MOMS, QPTS, LANES)).astype(np.float32)


def neighbours(ny, nz, nquad):
    quad, py, pz = lax.axis_index("quad"), lax.axis_index("py"), lax.axis_index("pz")
    parts = 2
    deep = (quad % parts) * nz + pz

    def in_group(dy, dz):
        return (quad, (py + dy + ny) % ny, (pz + dz + nz) % nz)

    def along_z(dz):
        at = (deep + dz + parts * nz) % (parts * nz)
        return (quad - quad % parts + at // nz, py, at % nz)

    return in_group, along_z


def group_offsets(ny, nz):
    every = [(a, b) for a in range(-ny // 2 + 1, ny // 2 + 1) for b in range(-nz // 2 + 1, nz // 2 + 1)]
    every = [o for o in every if o != (0, 0)]
    return sorted(every, key=lambda o: -(abs(o[0]) + 2 * abs(o[1])))


def kernel(
    ny, nz, nquad, sr, si, pot, center, radius, points, out,
    field, image, poten, table, packed, left, right, joint, packed_image, left_image,
    partial, received, moments,
    load_sem, ysend, yrecv, zsend, zrecv, y2send, y2recv, z2send, z2recv, asend, arecv,
):
    nsrc, cx, ry, _ = sr.shape
    slab = cx // nquad
    top = 8
    own = pl.ds(top, ry)
    low_halo, high_halo = pl.ds(top - REACH, REACH), pl.ds(top + ry, REACH)
    low_rows, high_rows = pl.ds(top, REACH), pl.ds(top + ry - REACH, REACH)
    in_group, along_z = neighbours(ny, nz, nquad)
    offsets = group_offsets(ny, nz)

    loads = []
    for s in range(nsrc):
        for c, ref in enumerate((sr, si)):
            copy = pltpu.make_async_copy(ref.at[s], field.at[s, c, :, own, :], load_sem.at[2 * s + c])
            copy.start()
            loads.append(copy)
    load_pot = pltpu.make_async_copy(pot, poten, load_sem.at[2 * nsrc])
    load_pot.start()
    load_table = pltpu.make_async_copy(points, table, load_sem.at[2 * nsrc + 1])
    load_table.start()

    barrier = pltpu.get_barrier_semaphore()
    for dz in (-1, 1):
        pl.semaphore_signal(barrier, inc=1, device_id=along_z(dz), device_id_type=MESH)
    for dy, dz in offsets[::-1]:
        pl.semaphore_signal(barrier, inc=1, device_id=in_group(dy, dz), device_id_type=MESH)

    lane = lax.broadcasted_iota(jnp.int32, (ry, LANES), 1)

    def pack(buf, s, to):
        for c in range(2):
            total = jnp.zeros((ry, LANES), jnp.float32)
            for x in range(cx):
                moved = pltpu.roll(buf[s, c, x, own, :], 8 * x + REACH, 1)
                total = jnp.where(lane // 8 == x, moved, total)
            to[s, c] = total

    for copy in loads:
        copy.wait()
    for s in range(nsrc):
        pack(field, s, packed)
    pl.semaphore_wait(barrier, len(offsets) + 2)

    for s in range(nsrc):
        pltpu.make_async_remote_copy(
            field.at[s, :, :, high_rows, :], field.at[s, :, :, low_halo, :],
            ysend.at[0], yrecv.at[2 * s], device_id=in_group(1, 0), device_id_type=MESH,
        ).start()
        pltpu.make_async_remote_copy(
            field.at[s, :, :, low_rows, :], field.at[s, :, :, high_halo, :],
            ysend.at[1], yrecv.at[2 * s + 1], device_id=in_group(-1, 0), device_id_type=MESH,
        ).start()
        pltpu.make_async_remote_copy(
            packed.at[s], left.at[s], zsend.at[0], zrecv.at[2 * s],
            device_id=along_z(1), device_id_type=MESH,
        ).start()
        pltpu.make_async_remote_copy(
            packed.at[s], right.at[s], zsend.at[1], zrecv.at[2 * s + 1],
            device_id=along_z(-1), device_id_type=MESH,
        ).start()

    load_pot.wait()
    load_table.wait()
    diagonal = 3.0 * half_weights[0] - center[0]
    zero = jnp.zeros((8, LANES), jnp.float32)

    def halves(value):
        total = value[0:8]
        for at in range(8, ry, 8):
            total = total + value[at : at + 8]
        return total

    def add_forms(sums, u, v):
        re = halves(u[0] * v[0] - u[1] * v[1])
        im = halves(u[0] * v[1] + u[1] * v[0])
        return (sums[0] + re, sums[1] + im)

    def keep(sums, quantity, s):
        partial[quantity, s] = sums

    def image_of(s):
        def step(x, sums):
            first, second, third = sums
            both = []
            for c in range(2):
                f = field[s, c, x, own, :]
                edge = pltpu.roll(joint[s, c], (LANES - REACH + (cx - x) * 8) % LANES, 1)
                total = (poten[x] + diagonal) * f
                for k in range(1, REACH + 1):
                    beside = field[s, c, (x + k) % cx, own, :] + field[s, c, (x + cx - k) % cx, own, :]
                    beside = beside + field[s, c, x, pl.ds(top - k, ry), :]
                    beside = beside + field[s, c, x, pl.ds(top + k, ry), :]
                    beside = beside + pltpu.roll(jnp.where(lane >= LANES - k, edge, f), k, 1)
                    beside = beside + pltpu.roll(jnp.where(lane < k, edge, f), LANES - k, 1)
                    total = total + half_weights[k] * beside
                image[s, c, x, own, :] = total
                both.append((f, total))
            u = (both[0][0], both[1][0])
            w = (both[0][1], both[1][1])
            return (add_forms(first, u, u), add_forms(second, u, w), add_forms(third, w, w))

        sums = lax.fori_loop(0, cx, step, ((zero, zero),) * 3, unroll=2)
        for i in range(3):
            for c in range(2):
                keep(sums[i][c], 2 * i + c, s)

    def last_form(s):
        sign = -1 if s < nsrc // 2 else 1

        def step(x, sums):
            w, once = [], []
            for c in range(2):
                f = image[s, c, x, own, :]
                edge = pltpu.roll(left_image[s, c], (LANES - REACH + (cx - x) * 8) % LANES, 1)
                total = (poten[x] + diagonal) * f
                for k in range(1, REACH + 1):
                    beside = image[s, c, (x + cx - k) % cx, own, :]
                    beside = beside + image[s, c, x, pl.ds(top + sign * k, ry), :]
                    beside = beside + pltpu.roll(jnp.where(lane >= LANES - k, edge, f), k, 1)
                    total = total + 2.0 * half_weights[k] * beside
                w.append(f)
                once.append(total)
            return add_forms(sums, w, once)

        sums = lax.fori_loop(0, cx, step, (zero, zero), unroll=2)
        for c in range(2):
            keep(sums[c], 6 + c, s)

    wide = field.at[0, :, :, low_halo, :]
    for s in range(nsrc):
        for sem in (yrecv.at[2 * s], yrecv.at[2 * s + 1]):
            pltpu.make_async_copy(wide, wide, sem).wait()
        for sem in (zrecv.at[2 * s], zrecv.at[2 * s + 1]):
            pltpu.make_async_copy(left.at[s], left.at[s], sem).wait()
        for c in range(2):
            joint[s, c] = jnp.where(lane % 8 < REACH, left[s, c], right[s, c])
        image_of(s)
        pack(image, s, packed_image)
        if s < nsrc // 2:
            pltpu.make_async_remote_copy(
                image.at[s, :, :, high_rows, :], image.at[s, :, :, low_halo, :],
                y2send, y2recv.at[s], device_id=in_group(1, 0), device_id_type=MESH,
            ).start()
        else:
            pltpu.make_async_remote_copy(
                image.at[s, :, :, low_rows, :], image.at[s, :, :, high_halo, :],
                y2send, y2recv.at[s], device_id=in_group(-1, 0), device_id_type=MESH,
            ).start()
        pltpu.make_async_remote_copy(
            packed_image.at[s], left_image.at[s], z2send, z2recv.at[s],
            device_id=along_z(1), device_id_type=MESH,
        ).start()

    spot = lax.broadcasted_iota(jnp.int32, (1, LANES), 1) // (LANES // (8 * nsrc))

    def gather_sums(quantities, row):
        for q in quantities:
            for s in range(nsrc):
                total = jnp.sum(partial[q, s], axis=0, keepdims=True)
                total = jnp.sum(total, axis=1, keepdims=True)
                row = jnp.where(spot == q * nsrc + s, total, row)
        return row

    row = gather_sums(range(6), jnp.zeros((1, LANES), jnp.float32))
    for s in range(nsrc):
        pltpu.make_async_copy(wide, wide, y2recv.at[s]).wait()
        pltpu.make_async_copy(left.at[s], left.at[s], z2recv.at[s]).wait()
        last_form(s)
    moments[...] = gather_sums(range(6, 8), row)

    for j, (dy, dz) in enumerate(offsets):
        pltpu.make_async_remote_copy(
            moments, received.at[j], asend, arecv, device_id=in_group(dy, dz), device_id_type=MESH,
        ).start()
    pltpu.make_async_copy(received, received, arecv).wait()
    total = moments[...]
    for j in range(len(offsets)):
        total = total + received[j]

    wide_total = jnp.broadcast_to(total, (QPTS, LANES))
    lanes_each = LANES // 8
    forms = [
        wide_total if q == 0 else pltpu.roll(wide_total, LANES - q * lanes_each, 1) for q in range(8)
    ]
    reach = radius[0]
    shift = (reach * table[0], reach * table[1])
    parts = coefficients([(forms[2 * i], forms[2 * i + 1]) for i in range(4)], shift)
    weights = {}
    for k in range(MOMS):
        factor = (reach * table[2 + 2 * k], reach * table[3 + 2 * k])
        for i, part in enumerate(parts):
            both = complex_mul(factor, part)
            for c in range(2):
                weights[k, i, c] = jnp.sum(both[c], axis=0, keepdims=True)

    first = lax.axis_index("quad") * slab
    write_output(out, field, image, weights, first, slab, own, nsrc)

    for i, halo in enumerate((low_halo, high_halo)):
        every = field.at[:, :, :, halo, :]
        pltpu.make_async_copy(every, every, ysend.at[i]).wait()
        pltpu.make_async_copy(packed, packed, zsend.at[i]).wait()
    every = image.at[:, :, :, low_halo, :]
    pltpu.make_async_copy(every, every, y2send).wait()
    pltpu.make_async_copy(packed_image, packed_image, z2send).wait()
    pltpu.make_async_copy(received, received, asend).wait()


def write_output(out, field, image, weights, first, slab, own, nsrc):
    for s in range(nsrc):
        lane_at = s * (LANES // (8 * nsrc))
        for k in range(MOMS):
            a = [weights[k, 0, c][:, lane_at : lane_at + 1] for c in range(2)]
            d = [weights[k, 1, c][:, lane_at : lane_at + 1] for c in range(2)]
            for x in range(slab):
                b = [field[s, c, first + x, own, :] for c in range(2)]
                w = [image[s, c, first + x, own, :] for c in range(2)]
                out[k, 0, s, x] = a[0] * b[0] - a[1] * b[1] + d[0] * w[0] - d[1] * w[1]
                out[k, 1, s, x] = a[0] * b[1] + a[1] * b[0] + d[0] * w[1] + d[1] * w[0]


def solution(mesh):
    nquad, ny, nz = mesh.shape["quad"], mesh.shape["py"], mesh.shape["pz"]

    def per_device(source_real, source_imag, potential, center, radius):
        nsrc, cx, ry, width = source_real.shape
        vmem, smem, hbm = pltpu.VMEM, pltpu.SMEM, pltpu.HBM
        padded = (nsrc, 2, cx, ry + 16, width)
        strips = (nsrc, 2, ry, width)
        peers = ny * nz - 1
        dma = pltpu.SemaphoreType.DMA
        f32 = jnp.float32

        def in_hbm(value):
            return pltpu.with_memory_space_constraint(value, hbm)

        return pl.pallas_call(
            functools.partial(kernel, ny, nz, nquad),
            out_shape=jax.ShapeDtypeStruct((MOMS, 2, nsrc, cx // nquad, ry, width), f32),
            in_specs=[
                pl.BlockSpec(memory_space=hbm),
                pl.BlockSpec(memory_space=hbm),
                pl.BlockSpec(memory_space=hbm),
                pl.BlockSpec(memory_space=smem),
                pl.BlockSpec(memory_space=smem),
                pl.BlockSpec(memory_space=hbm),
            ],
            out_specs=pl.BlockSpec(memory_space=vmem),
            scratch_shapes=[
                vmem(padded, f32), vmem(padded, f32), vmem((cx, ry, width), f32),
                vmem((2 + 2 * MOMS, QPTS, width), f32),
                vmem(strips, f32), vmem(strips, f32), vmem(strips, f32), vmem(strips, f32),
                vmem(strips, f32), vmem(strips, f32),
                vmem((8, nsrc, 8, width), f32), vmem((peers, 1, width), f32), vmem((1, width), f32),
                dma((2 * nsrc + 2,)), dma((2,)), dma((2 * nsrc,)), dma((2,)), dma((2 * nsrc,)),
                dma, dma((nsrc,)), dma, dma((nsrc,)), dma, dma,
            ],
            compiler_params=pltpu.CompilerParams(
                collective_id=0, has_side_effects=True, vmem_limit_bytes=32 * 1024 * 1024
            ),
        )(
            in_hbm(source_real), in_hbm(source_imag), in_hbm(potential), center, radius,
            in_hbm(jnp.asarray(tables())),
        )

    in_specs = (P(None, None, "py", "pz"), P(None, None, "py", "pz"), P(None, "py", "pz"), P(), P())
    out_specs = P(None, None, None, "quad", "py", "pz")
    return jax.shard_map(
        per_device, mesh=mesh, in_specs=in_specs, out_specs=out_specs, check_vma=False
    )
```

```python
import functools
import math

import jax
import jax.numpy as jnp
import numpy as np
from jax import lax
from jax.experimental import pallas as pl
from jax.experimental.pallas import tpu as pltpu
from jax.sharding import PartitionSpec as P

QPTS = 8
MOMS = 4
MESH = pl.DeviceIdType.MESH
LANES = 128
REACH = 4
stencil_weights = (-205.0 / 72.0, 8.0 / 5.0, -1.0 / 5.0, 8.0 / 315.0, -1.0 / 560.0)
half_weights = tuple(-0.5 * w for w in stencil_weights)


def complex_mul(left, right):
    return (left[0] * right[0] - left[1] * right[1], left[0] * right[1] + left[1] * right[0])


def complex_div(left, right):
    norm_sq = right[0] * right[0] + right[1] * right[1]
    return (
        (left[0] * right[0] + left[1] * right[1]) / norm_sq,
        (left[1] * right[0] - left[0] * right[1]) / norm_sq,
    )


def complex_sub(left, right):
    return (left[0] - right[0], left[1] - right[1])


def recip(value):
    norm_sq = value[0] * value[0] + value[1] * value[1]
    return (value[0] / norm_sq, -value[1] / norm_sq)


def coefficients(totals, shift):
    mu0, mu1, mu2, mu3 = totals
    tau = complex_div(mu1, mu0)
    tau_mu1 = complex_mul(tau, mu1)
    nu2 = complex_sub(mu2, tau_mu1)
    tau_mu2 = complex_mul(tau, mu2)
    nu3 = complex_sub(complex_sub(mu3, tau_mu2), complex_mul(tau, complex_sub(mu2, tau_mu1)))
    ratio = complex_div(nu3, nu2)
    slope = complex_div(nu2, mu0)
    alpha_first = recip(complex_sub(shift, tau))
    gamma = complex_mul(alpha_first, slope)
    alpha_next = recip(complex_sub(complex_sub(shift, ratio), gamma))
    image_part = complex_mul(alpha_first, alpha_next)
    back = complex_mul(image_part, complex_sub(gamma, tau))
    return (alpha_first[0] + back[0], alpha_first[1] + back[1]), image_part


def tables():
    theta = 2.0 * math.pi * (np.arange(QPTS) + 0.5) / QPTS
    rows = [np.cos(theta), np.sin(theta)]
    for k in range(1, MOMS + 1):
        rows += [np.cos(k * theta) / QPTS, np.sin(k * theta) / QPTS]
    return np.broadcast_to(np.stack(rows)[:, :, None], (2 + 2 * MOMS, QPTS, LANES)).astype(np.float32)


def neighbours(ny, nz, nquad):
    quad, py, pz = lax.axis_index("quad"), lax.axis_index("py"), lax.axis_index("pz")
    parts = 2
    deep = (quad % parts) * nz + pz

    def in_group(dy, dz):
        return (quad, (py + dy + ny) % ny, (pz + dz + nz) % nz)

    def along_z(dz):
        at = (deep + dz + parts * nz) % (parts * nz)
        return (quad - quad % parts + at // nz, py, at % nz)

    return in_group, along_z


def group_offsets(ny, nz):
    every = [(a, b) for a in range(-ny // 2 + 1, ny // 2 + 1) for b in range(-nz // 2 + 1, nz // 2 + 1)]
    every = [o for o in every if o != (0, 0)]
    return sorted(every, key=lambda o: -(abs(o[0]) + 2 * abs(o[1])))


def band(shape, one_sided):
    at = lax.broadcasted_iota(jnp.int32, shape, 0) % LANES
    to = lax.broadcasted_iota(jnp.int32, shape, 1)
    ahead = to % LANES - at
    value = jnp.zeros(shape, jnp.float32)
    for k in range(1, REACH + 1):
        hit = ahead == k if one_sided else jnp.abs(ahead) == k
        value = jnp.where(hit, (2.0 if one_sided else 1.0) * half_weights[k], value)
    high = value.astype(jnp.bfloat16)
    low = (value - high.astype(jnp.float32)).astype(jnp.bfloat16)
    return jnp.where(to < LANES, high.astype(jnp.float32), low.astype(jnp.float32)).astype(jnp.bfloat16)


def kernel(
    ny, nz, nquad, sr, si, pot, center, radius, points, out,
    field, image, halo, halo2, poten, table, packed, left, right, packed_image, left_image,
    split, zpart, two_sided, one_sided, partial, received, moments,
    load_sem, ysend, yrecv, zsend, zrecv, y2send, y2recv, z2send, z2recv, asend, arecv,
):
    nsrc, cx, ry, _ = sr.shape
    slab = cx // nquad
    half = cx // 2
    group = 4
    top = 8
    own = pl.ds(top, ry)
    low_halo, high_halo = pl.ds(top - REACH, REACH), pl.ds(top + ry, REACH)
    low_rows, high_rows = pl.ds(top, REACH), pl.ds(top + ry - REACH, REACH)
    in_group, along_z = neighbours(ny, nz, nquad)
    offsets = group_offsets(ny, nz)
    first_half, second_half = pl.ds(0, half), pl.ds(half, half)

    loads = []
    for s in range(nsrc):
        for c, ref in enumerate((sr, si)):
            copy = pltpu.make_async_copy(ref.at[s], field.at[s, c, :, own, :], load_sem.at[2 * s + c])
            copy.start()
            loads.append(copy)
    load_pot = pltpu.make_async_copy(pot, poten, load_sem.at[2 * nsrc])
    load_pot.start()
    load_table = pltpu.make_async_copy(points, table, load_sem.at[2 * nsrc + 1])
    load_table.start()

    barrier = pltpu.get_barrier_semaphore()
    for dz in (-1, 1):
        pl.semaphore_signal(barrier, inc=1, device_id=along_z(dz), device_id_type=MESH)
    for dy, dz in offsets[::-1]:
        pl.semaphore_signal(barrier, inc=1, device_id=in_group(dy, dz), device_id_type=MESH)

    lane = lax.broadcasted_iota(jnp.int32, (ry, LANES), 1)
    zero_tile = jnp.zeros((top, LANES), jnp.float32)
    zero = jnp.zeros((8, LANES), jnp.float32)

    def clear(i, carry):
        s = i // cx
        x = i % cx
        for c in range(2):
            for buf in (field, image):
                buf[s, c, x, pl.ds(0, top), :] = zero_tile
                buf[s, c, x, pl.ds(top + ry, top), :] = zero_tile
            for buf in (halo, halo2):
                for at in range(0, ry, top):
                    buf[s, c, x, pl.ds(top + at, top), :] = zero_tile
        return carry

    lax.fori_loop(0, nsrc * cx, clear, 0, unroll=2)
    two_sided[...] = band(two_sided.shape, False)
    one_sided[...] = band(one_sided.shape, True)

    for copy in loads:
        copy.wait()
    pl.semaphore_wait(barrier, len(offsets) + 2)

    for s in range(nsrc):
        pltpu.make_async_remote_copy(
            field.at[s, :, :, high_rows, :], halo.at[s, :, :, low_halo, :],
            ysend.at[0], yrecv.at[2 * s], device_id=in_group(1, 0), device_id_type=MESH,
        ).start()
        pltpu.make_async_remote_copy(
            field.at[s, :, :, low_rows, :], halo.at[s, :, :, high_halo, :],
            ysend.at[1], yrecv.at[2 * s + 1], device_id=in_group(-1, 0), device_id_type=MESH,
        ).start()

    def pack_into(buf, to, s):
        for c in range(2):
            total = jnp.zeros((ry, LANES), jnp.float32)
            for x in range(cx):
                moved = pltpu.roll(buf[s, c, x, own, :], 8 * x + REACH, 1)
                total = jnp.where(lane // 8 == x, moved, total)
            to[s, c] = total

    def pack(s, carry):
        pack_into(field, packed, s)
        pltpu.make_async_remote_copy(
            packed.at[s], left.at[s], zsend.at[0], zrecv.at[2 * s],
            device_id=along_z(1), device_id_type=MESH,
        ).start()
        pltpu.make_async_remote_copy(
            packed.at[s], right.at[s], zsend.at[1], zrecv.at[2 * s + 1],
            device_id=along_z(-1), device_id_type=MESH,
        ).start()
        return carry

    lax.fori_loop(0, nsrc, pack, 0)

    load_pot.wait()
    load_table.wait()
    diagonal = 3.0 * half_weights[0] - center[0]

    def halves(value):
        total = value[0:8]
        for at in range(8, ry, 8):
            total = total + value[at : at + 8]
        return total

    def add_forms(sums, u, v):
        re = halves(u[0] * v[0] - u[1] * v[1])
        im = halves(u[0] * v[1] + u[1] * v[0])
        return (sums[0] + re, sums[1] + im)

    def rows_of(c, x):
        return pl.ds(pl.multiple_of((c * cx + x) * ry, ry), ry)

    def put_split(c, x, value):
        high = value.astype(jnp.bfloat16)
        split[rows_of(c, x), 0:LANES] = high
        split[rows_of(c, x), LANES : 2 * LANES] = (value - high.astype(jnp.float32)).astype(jnp.bfloat16)

    def multiply(matrix):
        zpart[...] = jnp.dot(split[...], matrix[...], preferred_element_type=jnp.float32)

    def stage(buf, s):
        def step(g, carry):
            for i in range(group):
                for c in range(2):
                    put_split(c, g * group + i, buf[s, c, g * group + i, own, :])
            return carry

        lax.fori_loop(0, cx // group, step, 0)

    def along_lanes(c, x):
        return zpart[rows_of(c, x), 0:LANES] + zpart[rows_of(c, x), LANES : 2 * LANES]

    def local_image(s, carry):
        stage(field, s)
        multiply(two_sided)

        def step(g, carry):
            for i in range(group):
                x = g * group + i
                scale = poten[x] + diagonal
                for c in range(2):
                    total = scale * field[s, c, x, own, :] + along_lanes(c, x)
                    for k in range(1, REACH + 1):
                        beside = field[s, c, (x + k) % cx, own, :] + field[s, c, (x + cx - k) % cx, own, :]
                        beside = beside + field[s, c, x, pl.ds(top - k, ry), :]
                        beside = beside + field[s, c, x, pl.ds(top + k, ry), :]
                        total = total + half_weights[k] * beside
                    image[s, c, x, own, :] = total
            return carry

        lax.fori_loop(0, cx // group, step, 0)
        return carry

    lax.fori_loop(0, nsrc, local_image, 0)

    wide = field.at[0, :, :, low_halo, :]
    narrow = field.at[0, :, first_half, low_halo, :]
    tile_zero = jnp.zeros((ry, LANES), jnp.float32)
    low_part = lane % 8 < REACH
    at_edge = (lane < REACH) | (lane >= LANES - REACH)

    def finish(s, carry):
        for i in range(2):
            pltpu.make_async_copy(wide, wide, yrecv.at[2 * s + i]).wait()
            pltpu.make_async_copy(left.at[s], left.at[s], zrecv.at[2 * s + i]).wait()
        edges = []
        for c in range(2):
            below = jnp.where(low_part, left[s, c], 0.0)
            above = jnp.where(low_part, 0.0, right[s, c])
            total = tile_zero
            for k in range(1, REACH + 1):
                near = pltpu.roll(below, k, 1) * jnp.where(low_part, 0.0, half_weights[k])
                near = near + pltpu.roll(above, LANES - k, 1) * jnp.where(low_part, half_weights[k], 0.0)
                total = total + near
            edges.append(total)

        for x in range(cx):
            for c in range(2):
                f = image[s, c, x, own, :]
                moved = pltpu.roll(edges[c], (2 * LANES - REACH - 8 * x) % LANES, 1)
                down, up = zero, zero
                for k in range(1, REACH + 1):
                    down = down + half_weights[k] * halo[s, c, x, pl.ds(top - k, top), :]
                    up = up + half_weights[k] * halo[s, c, x, pl.ds(ry + k, top), :]
                image[s, c, x, own, :] = f + jnp.concatenate([down, up], 0) + jnp.where(at_edge, moved, 0.0)

        pltpu.make_async_remote_copy(
            image.at[s, :, first_half, high_rows, :], halo2.at[s, :, first_half, low_halo, :],
            y2send.at[0], y2recv.at[2 * s], device_id=in_group(1, 0), device_id_type=MESH,
        ).start()
        pltpu.make_async_remote_copy(
            image.at[s, :, second_half, low_rows, :], halo2.at[s, :, second_half, high_halo, :],
            y2send.at[1], y2recv.at[2 * s + 1], device_id=in_group(-1, 0), device_id_type=MESH,
        ).start()
        pack_into(image, packed_image, s)
        pltpu.make_async_remote_copy(
            packed_image.at[s], left_image.at[s], z2send, z2recv.at[s],
            device_id=along_z(1), device_id_type=MESH,
        ).start()

        stage(image, s)
        multiply(one_sided)
        sums = ((zero, zero),) * 4
        for upper in range(2):
            def pairs(g, sums):
                for i in range(group):
                    x = upper * half + g * group + i
                    scale = poten[x] + diagonal
                    b, w, once = [], [], []
                    for c in range(2):
                        f = image[s, c, x, own, :]
                        total = scale * f + along_lanes(c, x)
                        b.append(field[s, c, x, own, :])
                        for k in range(1, REACH + 1):
                            beside = image[s, c, (x + cx - k) % cx, own, :]
                            beside = beside + image[s, c, x, pl.ds(top + (k if upper else -k), ry), :]
                            total = total + 2.0 * half_weights[k] * beside
                        w.append(f)
                        once.append(total)
                    sides = ((b, b), (b, w), (w, w), (w, once))
                    sums = tuple(add_forms(old, *pair) for old, pair in zip(sums, sides))
                return sums

            sums = lax.fori_loop(0, half // group, pairs, sums)
        for i in range(4):
            for c in range(2):
                partial[2 * i + c, s] = sums[i][c]
        return carry

    lax.fori_loop(0, nsrc, finish, 0)

    spot = lax.broadcasted_iota(jnp.int32, (1, LANES), 1) // (LANES // (8 * nsrc))

    def gather_sums(quantities, row):
        for q in quantities:
            for s in range(nsrc):
                total = jnp.sum(partial[q, s], axis=0, keepdims=True)
                total = jnp.sum(total, axis=1, keepdims=True)
                row = jnp.where(spot == q * nsrc + s, total, row)
        return row

    row = gather_sums(range(6), jnp.zeros((1, LANES), jnp.float32))

    def across(s, carry):
        for i in range(2):
            pltpu.make_async_copy(narrow, narrow, y2recv.at[2 * s + i]).wait()
        pltpu.make_async_copy(left.at[s], left.at[s], z2recv.at[s]).wait()
        once = []
        for c in range(2):
            below = jnp.where(low_part, left_image[s, c], 0.0)
            total = tile_zero
            for k in range(1, REACH + 1):
                total = total + 2.0 * half_weights[k] * pltpu.roll(below, k, 1)
            once.append(jnp.where(low_part, 0.0, total))
        sums = add_forms((partial[6, s], partial[7, s]), (packed_image[s, 0], packed_image[s, 1]), once)
        for upper in range(2):
            def step(g, sums):
                for i in range(group):
                    x = upper * half + g * group + i
                    w, once = [], []
                    for c in range(2):
                        total = zero
                        for k in range(1, REACH + 1):
                            at = ry + k if upper else top - k
                            total = total + 2.0 * half_weights[k] * halo2[s, c, x, pl.ds(at, top), :]
                        once.append(total)
                        w.append(image[s, c, x, pl.ds(ry if upper else top, top), :])
                    re = w[0] * once[0] - w[1] * once[1]
                    im = w[0] * once[1] + w[1] * once[0]
                    sums = (sums[0] + re, sums[1] + im)
                return sums

            sums = lax.fori_loop(0, half // group, step, sums)
        for c in range(2):
            partial[6 + c, s] = sums[c]
        return carry

    lax.fori_loop(0, nsrc, across, 0)
    moments[...] = gather_sums(range(6, 8), row)

    for j, (dy, dz) in enumerate(offsets):
        pltpu.make_async_remote_copy(
            moments, received.at[j], asend, arecv, device_id=in_group(dy, dz), device_id_type=MESH,
        ).start()
    pltpu.make_async_copy(received, received, arecv).wait()
    total = moments[...]
    for j in range(len(offsets)):
        total = total + received[j]

    wide_total = jnp.broadcast_to(total, (QPTS, LANES))
    lanes_each = LANES // 8
    forms = [
        wide_total if q == 0 else pltpu.roll(wide_total, LANES - q * lanes_each, 1) for q in range(8)
    ]
    reach = radius[0]
    shift = (reach * table[0], reach * table[1])
    parts = coefficients([(forms[2 * i], forms[2 * i + 1]) for i in range(4)], shift)
    weights = {}
    for k in range(MOMS):
        factor = (reach * table[2 + 2 * k], reach * table[3 + 2 * k])
        for i, part in enumerate(parts):
            both = complex_mul(factor, part)
            for c in range(2):
                weights[k, i, c] = jnp.sum(both[c], axis=0, keepdims=True)

    first = lax.axis_index("quad") * slab
    write_output(out, field, image, weights, first, slab, own, nsrc)

    for i, strip in enumerate((low_halo, high_halo)):
        every = field.at[:, :, :, strip, :]
        pltpu.make_async_copy(every, every, ysend.at[i]).wait()
        pltpu.make_async_copy(packed, packed, zsend.at[i]).wait()
        every = image.at[:, :, first_half, strip, :]
        pltpu.make_async_copy(every, every, y2send.at[i]).wait()
    pltpu.make_async_copy(packed_image, packed_image, z2send).wait()
    pltpu.make_async_copy(received, received, asend).wait()


def write_output(out, field, image, weights, first, slab, own, nsrc):
    for s in range(nsrc):
        lane_at = s * (LANES // (8 * nsrc))
        for k in range(MOMS):
            a = [weights[k, 0, c][:, lane_at : lane_at + 1] for c in range(2)]
            d = [weights[k, 1, c][:, lane_at : lane_at + 1] for c in range(2)]
            for x in range(slab):
                b = [field[s, c, first + x, own, :] for c in range(2)]
                w = [image[s, c, first + x, own, :] for c in range(2)]
                out[k, 0, s, x] = a[0] * b[0] - a[1] * b[1] + d[0] * w[0] - d[1] * w[1]
                out[k, 1, s, x] = a[0] * b[1] + a[1] * b[0] + d[0] * w[1] + d[1] * w[0]


def solution(mesh):
    nquad, ny, nz = mesh.shape["quad"], mesh.shape["py"], mesh.shape["pz"]

    def per_device(source_real, source_imag, potential, center, radius):
        nsrc, cx, ry, width = source_real.shape
        vmem, smem, hbm = pltpu.VMEM, pltpu.SMEM, pltpu.HBM
        padded = (nsrc, 2, cx, ry + 16, width)
        strips = (nsrc, 2, ry, width)
        peers = ny * nz - 1
        dma = pltpu.SemaphoreType.DMA
        f32 = jnp.float32

        def in_hbm(value):
            return pltpu.with_memory_space_constraint(value, hbm)

        return pl.pallas_call(
            functools.partial(kernel, ny, nz, nquad),
            out_shape=jax.ShapeDtypeStruct((MOMS, 2, nsrc, cx // nquad, ry, width), f32),
            in_specs=[
                pl.BlockSpec(memory_space=hbm),
                pl.BlockSpec(memory_space=hbm),
                pl.BlockSpec(memory_space=hbm),
                pl.BlockSpec(memory_space=smem),
                pl.BlockSpec(memory_space=smem),
                pl.BlockSpec(memory_space=hbm),
            ],
            out_specs=pl.BlockSpec(memory_space=vmem),
            scratch_shapes=[
                vmem(padded, f32), vmem(padded, f32), vmem(padded, f32), vmem(padded, f32),
                vmem((cx, ry, width), f32), vmem((2 + 2 * MOMS, QPTS, width), f32),
                vmem(strips, f32), vmem(strips, f32), vmem(strips, f32), vmem(strips, f32), vmem(strips, f32),
                vmem((2 * cx * ry, 2 * width), jnp.bfloat16), vmem((2 * cx * ry, 2 * width), f32),
                vmem((2 * width, 2 * width), jnp.bfloat16), vmem((2 * width, 2 * width), jnp.bfloat16),
                vmem((8, nsrc, 8, width), f32), vmem((peers, 1, width), f32), vmem((1, width), f32),
                dma((2 * nsrc + 2,)), dma((2,)), dma((2 * nsrc,)), dma((2,)), dma((2 * nsrc,)),
                dma((2,)), dma((2 * nsrc,)), dma, dma((nsrc,)), dma, dma,
            ],
            compiler_params=pltpu.CompilerParams(
                collective_id=0, has_side_effects=True, vmem_limit_bytes=32 * 1024 * 1024
            ),
        )(
            in_hbm(source_real), in_hbm(source_imag), in_hbm(potential), center, radius,
            in_hbm(jnp.asarray(tables())),
        )

    in_specs = (P(None, None, "py", "pz"), P(None, None, "py", "pz"), P(None, "py", "pz"), P(), P())
    out_specs = P(None, None, None, "quad", "py", "pz")
    return jax.shard_map(
        per_device, mesh=mesh, in_specs=in_specs, out_specs=out_specs, check_vma=False
    )
```

```python
import functools
import math

import jax
import jax.numpy as jnp
import numpy as np
from jax import lax
from jax.experimental import pallas as pl
from jax.experimental.pallas import tpu as pltpu
from jax.sharding import PartitionSpec as P

QPTS = 8
MOMS = 4
MESH = pl.DeviceIdType.MESH
LANES = 128
REACH = 4
stencil_weights = (-205.0 / 72.0, 8.0 / 5.0, -1.0 / 5.0, 8.0 / 315.0, -1.0 / 560.0)
half_weights = tuple(-0.5 * w for w in stencil_weights)


def complex_mul(left, right):
    return (left[0] * right[0] - left[1] * right[1], left[0] * right[1] + left[1] * right[0])


def complex_div(left, right):
    norm_sq = right[0] * right[0] + right[1] * right[1]
    return (
        (left[0] * right[0] + left[1] * right[1]) / norm_sq,
        (left[1] * right[0] - left[0] * right[1]) / norm_sq,
    )


def complex_sub(left, right):
    return (left[0] - right[0], left[1] - right[1])


def recip(value):
    norm_sq = value[0] * value[0] + value[1] * value[1]
    return (value[0] / norm_sq, -value[1] / norm_sq)


def coefficients(totals, shift):
    mu0, mu1, mu2, mu3 = totals
    tau = complex_div(mu1, mu0)
    tau_mu1 = complex_mul(tau, mu1)
    nu2 = complex_sub(mu2, tau_mu1)
    tau_mu2 = complex_mul(tau, mu2)
    nu3 = complex_sub(complex_sub(mu3, tau_mu2), complex_mul(tau, complex_sub(mu2, tau_mu1)))
    ratio = complex_div(nu3, nu2)
    slope = complex_div(nu2, mu0)
    alpha_first = recip(complex_sub(shift, tau))
    gamma = complex_mul(alpha_first, slope)
    alpha_next = recip(complex_sub(complex_sub(shift, ratio), gamma))
    image_part = complex_mul(alpha_first, alpha_next)
    back = complex_mul(image_part, complex_sub(gamma, tau))
    return (alpha_first[0] + back[0], alpha_first[1] + back[1]), image_part


def tables():
    theta = 2.0 * math.pi * (np.arange(QPTS) + 0.5) / QPTS
    rows = [np.cos(theta), np.sin(theta)]
    for k in range(1, MOMS + 1):
        rows += [np.cos(k * theta) / QPTS, np.sin(k * theta) / QPTS]
    return np.broadcast_to(np.stack(rows)[:, :, None], (2 + 2 * MOMS, QPTS, LANES)).astype(np.float32)


BESIDE = ((1, 0), (-1, 0), (0, 1), (0, -1))
RELAY = (BESIDE, ((2, 0), (-2, 0), (0, 2), (0, -2)), ((4, 0), (0, 3), (0, -3)))


def neighbours(ny, nz, nquad):
    quad, py, pz = lax.axis_index("quad"), lax.axis_index("py"), lax.axis_index("pz")
    parts = 2
    deep = (quad % parts) * nz + pz

    def in_group(dy, dz):
        return (quad, (py + dy + ny) % ny, (pz + dz + nz) % nz)

    def along(dy, dz):
        at = (deep + dz + parts * nz) % (parts * nz)
        return (quad - quad % parts + at // nz, (py + dy + ny) % ny, at % nz)

    return in_group, along


def group_offsets(ny, nz):
    every = [(a, b) for a in range(-ny // 2 + 1, ny // 2 + 1) for b in range(-nz // 2 + 1, nz // 2 + 1)]
    every = [o for o in every if o != (0, 0)]
    return sorted(every, key=lambda o: -(abs(o[0]) + 2 * abs(o[1])))


def band(shape, one_sided):
    at = lax.broadcasted_iota(jnp.int32, shape, 0) % LANES
    to = lax.broadcasted_iota(jnp.int32, shape, 1)
    ahead = to % LANES - at
    value = jnp.zeros(shape, jnp.float32)
    for k in range(1, REACH + 1):
        hit = ahead == k if one_sided else jnp.abs(ahead) == k
        value = jnp.where(hit, (2.0 if one_sided else 1.0) * half_weights[k], value)
    high = value.astype(jnp.bfloat16)
    low = (value - high.astype(jnp.float32)).astype(jnp.bfloat16)
    return jnp.where(to < LANES, high.astype(jnp.float32), low.astype(jnp.float32)).astype(jnp.bfloat16)


def kernel(
    ny, nz, nquad, sr, si, pot, center, radius, points, out,
    field, image, halo, halo2, poten, table, packed, left, right, packed_image, left_image,
    split, zpart, two_sided, one_sided, partial, received, moments,
    load_sem, ysend, yrecv, zsend, zrecv, y2send, y2recv, z2send, z2recv, asend, arecv, entered,
):
    nsrc, cx, ry, _ = sr.shape
    slab = cx // nquad
    half = cx // 2
    group = 4
    top = 8
    own = pl.ds(top, ry)
    low_halo, high_halo = pl.ds(top - REACH, REACH), pl.ds(top + ry, REACH)
    low_rows, high_rows = pl.ds(top, REACH), pl.ds(top + ry - REACH, REACH)
    in_group, along = neighbours(ny, nz, nquad)
    offsets = group_offsets(ny, nz)
    first_half, second_half = pl.ds(0, half), pl.ds(half, half)

    loads = []
    for s in range(nsrc):
        for c, ref in enumerate((sr, si)):
            copy = pltpu.make_async_copy(ref.at[s], field.at[s, c, :, own, :], load_sem.at[2 * s + c])
            copy.start()
            loads.append(copy)
    load_pot = pltpu.make_async_copy(pot, poten, load_sem.at[2 * nsrc])
    load_pot.start()
    load_table = pltpu.make_async_copy(points, table, load_sem.at[2 * nsrc + 1])
    load_table.start()

    barrier = pltpu.get_barrier_semaphore()
    for dy, dz in BESIDE:
        pl.semaphore_signal(barrier, inc=1, device_id=along(dy, dz), device_id_type=MESH)

    def pass_on(stage_at):
        for dy, dz in RELAY[stage_at]:
            pl.semaphore_signal(
                entered.at[stage_at], inc=1, device_id=along(dy, dz), device_id_type=MESH
            )

    def hear(stage_at):
        pl.semaphore_wait(entered.at[stage_at], len(RELAY[stage_at]))

    lane = lax.broadcasted_iota(jnp.int32, (ry, LANES), 1)
    zero_tile = jnp.zeros((top, LANES), jnp.float32)
    zero = jnp.zeros((8, LANES), jnp.float32)

    def clear(i, carry):
        s = i // cx
        x = i % cx
        for c in range(2):
            for buf in (field, image):
                buf[s, c, x, pl.ds(0, top), :] = zero_tile
                buf[s, c, x, pl.ds(top + ry, top), :] = zero_tile
            for buf in (halo, halo2):
                for at in range(0, ry, top):
                    buf[s, c, x, pl.ds(top + at, top), :] = zero_tile
        return carry

    lax.fori_loop(0, nsrc * cx, clear, 0, unroll=2)
    two_sided[...] = band(two_sided.shape, False)
    one_sided[...] = band(one_sided.shape, True)

    for copy in loads:
        copy.wait()
    pl.semaphore_wait(barrier, len(BESIDE))

    for s in range(nsrc):
        pltpu.make_async_remote_copy(
            field.at[s, :, :, high_rows, :], halo.at[s, :, :, low_halo, :],
            ysend.at[0], yrecv.at[2 * s], device_id=in_group(1, 0), device_id_type=MESH,
        ).start()
        pltpu.make_async_remote_copy(
            field.at[s, :, :, low_rows, :], halo.at[s, :, :, high_halo, :],
            ysend.at[1], yrecv.at[2 * s + 1], device_id=in_group(-1, 0), device_id_type=MESH,
        ).start()

    def pack_into(buf, to, s):
        for c in range(2):
            total = jnp.zeros((ry, LANES), jnp.float32)
            for x in range(cx):
                moved = pltpu.roll(buf[s, c, x, own, :], 8 * x + REACH, 1)
                total = jnp.where(lane // 8 == x, moved, total)
            to[s, c] = total

    def pack(s, carry):
        pack_into(field, packed, s)
        pltpu.make_async_remote_copy(
            packed.at[s], left.at[s], zsend.at[0], zrecv.at[2 * s],
            device_id=along(0, 1), device_id_type=MESH,
        ).start()
        pltpu.make_async_remote_copy(
            packed.at[s], right.at[s], zsend.at[1], zrecv.at[2 * s + 1],
            device_id=along(0, -1), device_id_type=MESH,
        ).start()
        return carry

    lax.fori_loop(0, nsrc, pack, 0)
    pass_on(0)

    load_pot.wait()
    load_table.wait()
    diagonal = 3.0 * half_weights[0] - center[0]

    def halves(value):
        total = value[0:8]
        for at in range(8, ry, 8):
            total = total + value[at : at + 8]
        return total

    def add_forms(sums, u, v):
        re = halves(u[0] * v[0] - u[1] * v[1])
        im = halves(u[0] * v[1] + u[1] * v[0])
        return (sums[0] + re, sums[1] + im)

    def rows_of(c, x):
        return pl.ds(pl.multiple_of((c * cx + x) * ry, ry), ry)

    def put_split(c, x, value):
        high = value.astype(jnp.bfloat16)
        split[rows_of(c, x), 0:LANES] = high
        split[rows_of(c, x), LANES : 2 * LANES] = (value - high.astype(jnp.float32)).astype(jnp.bfloat16)

    def multiply(matrix):
        zpart[...] = jnp.dot(split[...], matrix[...], preferred_element_type=jnp.float32)

    def stage(buf, s):
        def step(g, carry):
            for i in range(group):
                for c in range(2):
                    put_split(c, g * group + i, buf[s, c, g * group + i, own, :])
            return carry

        lax.fori_loop(0, cx // group, step, 0)

    def along_lanes(c, x):
        return zpart[rows_of(c, x), 0:LANES] + zpart[rows_of(c, x), LANES : 2 * LANES]

    def local_image(s, carry):
        stage(field, s)
        multiply(two_sided)

        def step(g, carry):
            for i in range(group):
                x = g * group + i
                scale = poten[x] + diagonal
                for c in range(2):
                    total = scale * field[s, c, x, own, :] + along_lanes(c, x)
                    for k in range(1, REACH + 1):
                        beside = field[s, c, (x + k) % cx, own, :] + field[s, c, (x + cx - k) % cx, own, :]
                        beside = beside + field[s, c, x, pl.ds(top - k, ry), :]
                        beside = beside + field[s, c, x, pl.ds(top + k, ry), :]
                        total = total + half_weights[k] * beside
                    image[s, c, x, own, :] = total
            return carry

        lax.fori_loop(0, cx // group, step, 0)
        return carry

    lax.fori_loop(0, nsrc, local_image, 0)
    hear(0)
    pass_on(1)

    wide = field.at[0, :, :, low_halo, :]
    narrow = field.at[0, :, first_half, low_halo, :]
    tile_zero = jnp.zeros((ry, LANES), jnp.float32)
    low_part = lane % 8 < REACH
    at_edge = (lane < REACH) | (lane >= LANES - REACH)

    def finish(s, carry):
        for i in range(2):
            pltpu.make_async_copy(wide, wide, yrecv.at[2 * s + i]).wait()
            pltpu.make_async_copy(left.at[s], left.at[s], zrecv.at[2 * s + i]).wait()
        edges = []
        for c in range(2):
            below = jnp.where(low_part, left[s, c], 0.0)
            above = jnp.where(low_part, 0.0, right[s, c])
            total = tile_zero
            for k in range(1, REACH + 1):
                near = pltpu.roll(below, k, 1) * jnp.where(low_part, 0.0, half_weights[k])
                near = near + pltpu.roll(above, LANES - k, 1) * jnp.where(low_part, half_weights[k], 0.0)
                total = total + near
            edges.append(total)

        for x in range(cx):
            for c in range(2):
                f = image[s, c, x, own, :]
                moved = pltpu.roll(edges[c], (2 * LANES - REACH - 8 * x) % LANES, 1)
                down, up = zero, zero
                for k in range(1, REACH + 1):
                    down = down + half_weights[k] * halo[s, c, x, pl.ds(top - k, top), :]
                    up = up + half_weights[k] * halo[s, c, x, pl.ds(ry + k, top), :]
                image[s, c, x, own, :] = f + jnp.concatenate([down, up], 0) + jnp.where(at_edge, moved, 0.0)

        pltpu.make_async_remote_copy(
            image.at[s, :, first_half, high_rows, :], halo2.at[s, :, first_half, low_halo, :],
            y2send.at[0], y2recv.at[2 * s], device_id=in_group(1, 0), device_id_type=MESH,
        ).start()
        pltpu.make_async_remote_copy(
            image.at[s, :, second_half, low_rows, :], halo2.at[s, :, second_half, high_halo, :],
            y2send.at[1], y2recv.at[2 * s + 1], device_id=in_group(-1, 0), device_id_type=MESH,
        ).start()
        pack_into(image, packed_image, s)
        pltpu.make_async_remote_copy(
            packed_image.at[s], left_image.at[s], z2send, z2recv.at[s],
            device_id=along(0, 1), device_id_type=MESH,
        ).start()

        stage(image, s)
        multiply(one_sided)
        sums = ((zero, zero),) * 4
        for upper in range(2):
            def pairs(g, sums):
                for i in range(group):
                    x = upper * half + g * group + i
                    scale = poten[x] + diagonal
                    b, w, once = [], [], []
                    for c in range(2):
                        f = image[s, c, x, own, :]
                        total = scale * f + along_lanes(c, x)
                        b.append(field[s, c, x, own, :])
                        for k in range(1, REACH + 1):
                            beside = image[s, c, (x + cx - k) % cx, own, :]
                            beside = beside + image[s, c, x, pl.ds(top + (k if upper else -k), ry), :]
                            total = total + 2.0 * half_weights[k] * beside
                        w.append(f)
                        once.append(total)
                    sides = ((b, b), (b, w), (w, w), (w, once))
                    sums = tuple(add_forms(old, *pair) for old, pair in zip(sums, sides))
                return sums

            sums = lax.fori_loop(0, half // group, pairs, sums)
        for i in range(4):
            for c in range(2):
                partial[2 * i + c, s] = sums[i][c]
        return carry

    lax.fori_loop(0, nsrc, finish, 0)
    hear(1)
    pass_on(2)

    spot = lax.broadcasted_iota(jnp.int32, (1, LANES), 1) // (LANES // (8 * nsrc))

    def gather_sums(quantities, row):
        for q in quantities:
            for s in range(nsrc):
                total = jnp.sum(partial[q, s], axis=0, keepdims=True)
                total = jnp.sum(total, axis=1, keepdims=True)
                row = jnp.where(spot == q * nsrc + s, total, row)
        return row

    row = gather_sums(range(6), jnp.zeros((1, LANES), jnp.float32))

    def across(s, carry):
        for i in range(2):
            pltpu.make_async_copy(narrow, narrow, y2recv.at[2 * s + i]).wait()
        pltpu.make_async_copy(left.at[s], left.at[s], z2recv.at[s]).wait()
        once = []
        for c in range(2):
            below = jnp.where(low_part, left_image[s, c], 0.0)
            total = tile_zero
            for k in range(1, REACH + 1):
                total = total + 2.0 * half_weights[k] * pltpu.roll(below, k, 1)
            once.append(jnp.where(low_part, 0.0, total))
        sums = add_forms((partial[6, s], partial[7, s]), (packed_image[s, 0], packed_image[s, 1]), once)
        for upper in range(2):
            def step(g, sums):
                for i in range(group):
                    x = upper * half + g * group + i
                    w, once = [], []
                    for c in range(2):
                        total = zero
                        for k in range(1, REACH + 1):
                            at = ry + k if upper else top - k
                            total = total + 2.0 * half_weights[k] * halo2[s, c, x, pl.ds(at, top), :]
                        once.append(total)
                        w.append(image[s, c, x, pl.ds(ry if upper else top, top), :])
                    re = w[0] * once[0] - w[1] * once[1]
                    im = w[0] * once[1] + w[1] * once[0]
                    sums = (sums[0] + re, sums[1] + im)
                return sums

            sums = lax.fori_loop(0, half // group, step, sums)
        for c in range(2):
            partial[6 + c, s] = sums[c]
        return carry

    lax.fori_loop(0, nsrc, across, 0)
    moments[...] = gather_sums(range(6, 8), row)
    hear(2)

    for j, (dy, dz) in enumerate(offsets):
        pltpu.make_async_remote_copy(
            moments, received.at[j], asend, arecv, device_id=in_group(dy, dz), device_id_type=MESH,
        ).start()
    pltpu.make_async_copy(received, received, arecv).wait()
    total = moments[...]
    for j in range(len(offsets)):
        total = total + received[j]

    wide_total = jnp.broadcast_to(total, (QPTS, LANES))
    lanes_each = LANES // 8
    forms = [
        wide_total if q == 0 else pltpu.roll(wide_total, LANES - q * lanes_each, 1) for q in range(8)
    ]
    reach = radius[0]
    shift = (reach * table[0], reach * table[1])
    parts = coefficients([(forms[2 * i], forms[2 * i + 1]) for i in range(4)], shift)
    weights = {}
    for k in range(MOMS):
        factor = (reach * table[2 + 2 * k], reach * table[3 + 2 * k])
        for i, part in enumerate(parts):
            both = complex_mul(factor, part)
            for c in range(2):
                weights[k, i, c] = jnp.sum(both[c], axis=0, keepdims=True)

    first = lax.axis_index("quad") * slab
    write_output(out, field, image, weights, first, slab, own, nsrc)

    for i, strip in enumerate((low_halo, high_halo)):
        every = field.at[:, :, :, strip, :]
        pltpu.make_async_copy(every, every, ysend.at[i]).wait()
        pltpu.make_async_copy(packed, packed, zsend.at[i]).wait()
        every = image.at[:, :, first_half, strip, :]
        pltpu.make_async_copy(every, every, y2send.at[i]).wait()
    pltpu.make_async_copy(packed_image, packed_image, z2send).wait()
    pltpu.make_async_copy(received, received, asend).wait()


def write_output(out, field, image, weights, first, slab, own, nsrc):
    for s in range(nsrc):
        lane_at = s * (LANES // (8 * nsrc))
        for k in range(MOMS):
            a = [weights[k, 0, c][:, lane_at : lane_at + 1] for c in range(2)]
            d = [weights[k, 1, c][:, lane_at : lane_at + 1] for c in range(2)]
            for x in range(slab):
                b = [field[s, c, first + x, own, :] for c in range(2)]
                w = [image[s, c, first + x, own, :] for c in range(2)]
                out[k, 0, s, x] = a[0] * b[0] - a[1] * b[1] + d[0] * w[0] - d[1] * w[1]
                out[k, 1, s, x] = a[0] * b[1] + a[1] * b[0] + d[0] * w[1] + d[1] * w[0]


def solution(mesh):
    nquad, ny, nz = mesh.shape["quad"], mesh.shape["py"], mesh.shape["pz"]

    def per_device(source_real, source_imag, potential, center, radius):
        nsrc, cx, ry, width = source_real.shape
        vmem, smem, hbm = pltpu.VMEM, pltpu.SMEM, pltpu.HBM
        padded = (nsrc, 2, cx, ry + 16, width)
        strips = (nsrc, 2, ry, width)
        peers = ny * nz - 1
        dma = pltpu.SemaphoreType.DMA
        f32 = jnp.float32

        def in_hbm(value):
            return pltpu.with_memory_space_constraint(value, hbm)

        return pl.pallas_call(
            functools.partial(kernel, ny, nz, nquad),
            out_shape=jax.ShapeDtypeStruct((MOMS, 2, nsrc, cx // nquad, ry, width), f32),
            in_specs=[
                pl.BlockSpec(memory_space=hbm),
                pl.BlockSpec(memory_space=hbm),
                pl.BlockSpec(memory_space=hbm),
                pl.BlockSpec(memory_space=smem),
                pl.BlockSpec(memory_space=smem),
                pl.BlockSpec(memory_space=hbm),
            ],
            out_specs=pl.BlockSpec(memory_space=vmem),
            scratch_shapes=[
                vmem(padded, f32), vmem(padded, f32), vmem(padded, f32), vmem(padded, f32),
                vmem((cx, ry, width), f32), vmem((2 + 2 * MOMS, QPTS, width), f32),
                vmem(strips, f32), vmem(strips, f32), vmem(strips, f32), vmem(strips, f32), vmem(strips, f32),
                vmem((2 * cx * ry, 2 * width), jnp.bfloat16), vmem((2 * cx * ry, 2 * width), f32),
                vmem((2 * width, 2 * width), jnp.bfloat16), vmem((2 * width, 2 * width), jnp.bfloat16),
                vmem((8, nsrc, 8, width), f32), vmem((peers, 1, width), f32), vmem((1, width), f32),
                dma((2 * nsrc + 2,)), dma((2,)), dma((2 * nsrc,)), dma((2,)), dma((2 * nsrc,)),
                dma((2,)), dma((2 * nsrc,)), dma, dma((nsrc,)), dma, dma,
                pltpu.SemaphoreType.REGULAR((len(RELAY),)),
            ],
            compiler_params=pltpu.CompilerParams(
                collective_id=0, has_side_effects=True, vmem_limit_bytes=32 * 1024 * 1024
            ),
        )(
            in_hbm(source_real), in_hbm(source_imag), in_hbm(potential), center, radius,
            in_hbm(jnp.asarray(tables())),
        )

    in_specs = (P(None, None, "py", "pz"), P(None, None, "py", "pz"), P(None, "py", "pz"), P(), P())
    out_specs = P(None, None, None, "quad", "py", "pz")
    return jax.shard_map(
        per_device, mesh=mesh, in_specs=in_specs, out_specs=out_specs, check_vma=False
    )
```

```python
import functools
import math

import jax
import jax.numpy as jnp
import numpy as np
from jax import lax
from jax.experimental import pallas as pl
from jax.experimental.pallas import tpu as pltpu
from jax.sharding import PartitionSpec as P

QPTS = 8
MOMS = 4
MESH = pl.DeviceIdType.MESH
LANES = 128
REACH = 4
stencil_weights = (-205.0 / 72.0, 8.0 / 5.0, -1.0 / 5.0, 8.0 / 315.0, -1.0 / 560.0)
half_weights = tuple(-0.5 * w for w in stencil_weights)


def complex_mul(left, right):
    return (left[0] * right[0] - left[1] * right[1], left[0] * right[1] + left[1] * right[0])


def complex_div(left, right):
    norm_sq = right[0] * right[0] + right[1] * right[1]
    return (
        (left[0] * right[0] + left[1] * right[1]) / norm_sq,
        (left[1] * right[0] - left[0] * right[1]) / norm_sq,
    )


def complex_sub(left, right):
    return (left[0] - right[0], left[1] - right[1])


def recip(value):
    norm_sq = value[0] * value[0] + value[1] * value[1]
    return (value[0] / norm_sq, -value[1] / norm_sq)


def coefficients(totals, shift):
    mu0, mu1, mu2, mu3 = totals
    tau = complex_div(mu1, mu0)
    tau_mu1 = complex_mul(tau, mu1)
    nu2 = complex_sub(mu2, tau_mu1)
    tau_mu2 = complex_mul(tau, mu2)
    nu3 = complex_sub(complex_sub(mu3, tau_mu2), complex_mul(tau, complex_sub(mu2, tau_mu1)))
    ratio = complex_div(nu3, nu2)
    slope = complex_div(nu2, mu0)
    alpha_first = recip(complex_sub(shift, tau))
    gamma = complex_mul(alpha_first, slope)
    alpha_next = recip(complex_sub(complex_sub(shift, ratio), gamma))
    image_part = complex_mul(alpha_first, alpha_next)
    back = complex_mul(image_part, complex_sub(gamma, tau))
    return (alpha_first[0] + back[0], alpha_first[1] + back[1]), image_part


def tables():
    theta = 2.0 * math.pi * (np.arange(QPTS) + 0.5) / QPTS
    rows = [np.cos(theta), np.sin(theta)]
    for k in range(1, MOMS + 1):
        rows += [np.cos(k * theta) / QPTS, np.sin(k * theta) / QPTS]
    return np.broadcast_to(np.stack(rows)[:, :, None], (2 + 2 * MOMS, QPTS, LANES)).astype(np.float32)


BESIDE = ((1, 0), (-1, 0), (0, 1), (0, -1))
RELAY = (BESIDE, ((2, 0), (-2, 0), (0, 2)), ((4, 0),))


def group_offsets(ny, nz):
    every = [(a, b) for a in range(-ny // 2 + 1, ny // 2 + 1) for b in range(-nz // 2 + 1, nz // 2 + 1)]
    every = [o for o in every if o != (0, 0)]
    return sorted(every, key=lambda o: -(abs(o[0]) + 2 * abs(o[1])))


def band(shape, one_sided):
    at = lax.broadcasted_iota(jnp.int32, shape, 0) % LANES
    to = lax.broadcasted_iota(jnp.int32, shape, 1)
    ahead = to % LANES - at
    value = jnp.zeros(shape, jnp.float32)
    for k in range(1, REACH + 1):
        hit = ahead == k if one_sided else jnp.abs(ahead) == k
        value = jnp.where(hit, (2.0 if one_sided else 1.0) * half_weights[k], value)
    high = value.astype(jnp.bfloat16)
    low = (value - high.astype(jnp.float32)).astype(jnp.bfloat16)
    return jnp.where(to < LANES, high.astype(jnp.float32), low.astype(jnp.float32)).astype(jnp.bfloat16)


def kernel(
    ny, nz, nquad, sr, si, pot, center, radius, points, out,
    field, image, halo, halo2, poten, table, up, down, left, right, image_strip, image_up, left_image,
    split, zpart, two_sided, one_sided, partial, received, moments,
    load_sem, ysend, yrecv, zsend, zrecv, y2send, y2recv, z2send, z2recv, asend, arecv, entered,
):
    nsrc, cx, ry, _ = sr.shape
    slab = cx // nquad
    half = cx // 2
    group = 4
    top = 8
    own = pl.ds(top, ry)
    low_halo, high_halo = pl.ds(top - REACH, REACH), pl.ds(top + ry, REACH)
    low_rows, high_rows = pl.ds(top, REACH), pl.ds(top + ry - REACH, REACH)
    quad, py, pz = lax.axis_index("quad"), lax.axis_index("py"), lax.axis_index("pz")

    def in_group(dy, dz):
        return (quad, (py + dy + ny) % ny, (pz + dz + nz) % nz)

    offsets = group_offsets(ny, nz)
    first_half, second_half = pl.ds(0, half), pl.ds(half, half)

    loads = []
    for s in range(nsrc):
        for c, ref in enumerate((sr, si)):
            copy = pltpu.make_async_copy(ref.at[s], field.at[s, c, :, own, :], load_sem.at[2 * s + c])
            copy.start()
            loads.append(copy)
    load_pot = pltpu.make_async_copy(pot, poten, load_sem.at[2 * nsrc])
    load_pot.start()
    load_table = pltpu.make_async_copy(points, table, load_sem.at[2 * nsrc + 1])
    load_table.start()

    barrier = pltpu.get_barrier_semaphore()
    for dy, dz in BESIDE:
        pl.semaphore_signal(barrier, inc=1, device_id=in_group(dy, dz), device_id_type=MESH)

    def pass_on(stage_at):
        for dy, dz in RELAY[stage_at]:
            pl.semaphore_signal(
                entered.at[stage_at], inc=1, device_id=in_group(dy, dz), device_id_type=MESH
            )

    def hear(stage_at):
        pl.semaphore_wait(entered.at[stage_at], len(RELAY[stage_at]))

    lane = lax.broadcasted_iota(jnp.int32, (ry, LANES), 1)
    zero_tile = jnp.zeros((top, LANES), jnp.float32)
    zero = jnp.zeros((8, LANES), jnp.float32)

    def clear(i, carry):
        s = i // cx
        x = i % cx
        for c in range(2):
            for buf in (field, image):
                buf[s, c, x, pl.ds(0, top), :] = zero_tile
                buf[s, c, x, pl.ds(top + ry, top), :] = zero_tile
            for buf in (halo, halo2):
                for at in range(0, ry, top):
                    buf[s, c, x, pl.ds(top + at, top), :] = zero_tile
        return carry

    lax.fori_loop(0, nsrc * cx, clear, 0, unroll=2)
    two_sided[...] = band(two_sided.shape, False)
    one_sided[...] = band(one_sided.shape, True)

    for copy in loads:
        copy.wait()
    low_part = lane % 8 < REACH

    def strips_of(buf, s):
        parts = []
        for c in range(2):
            total = jnp.zeros((ry, LANES), jnp.float32)
            for x in range(cx):
                moved = pltpu.roll(buf[s, c, x, own, :], 8 * x + REACH, 1)
                total = jnp.where(lane // 8 == x, moved, total)
            parts.append(total)
        return parts

    def last_lanes(parts):
        return jnp.where(low_part, parts[0], pltpu.roll(parts[1], REACH, 1))

    def from_last(both):
        return [jnp.where(low_part, t, 0.0) for t in (both, pltpu.roll(both, LANES - REACH, 1))]

    def pack(s, carry):
        parts = strips_of(field, s)
        up[s] = last_lanes(parts)
        down[s] = jnp.where(low_part, pltpu.roll(parts[0], LANES - REACH, 1), parts[1])
        return carry

    lax.fori_loop(0, nsrc, pack, 0)
    pl.semaphore_wait(barrier, len(BESIDE))

    for s in range(nsrc):
        pltpu.make_async_remote_copy(
            up.at[s], left.at[s], zsend.at[0], zrecv.at[2 * s],
            device_id=in_group(0, 1), device_id_type=MESH,
        ).start()
        pltpu.make_async_remote_copy(
            down.at[s], right.at[s], zsend.at[1], zrecv.at[2 * s + 1],
            device_id=in_group(0, -1), device_id_type=MESH,
        ).start()

    for s in range(nsrc):
        pltpu.make_async_remote_copy(
            field.at[s, :, :, high_rows, :], halo.at[s, :, :, low_halo, :],
            ysend.at[0], yrecv.at[2 * s], device_id=in_group(1, 0), device_id_type=MESH,
        ).start()
        pltpu.make_async_remote_copy(
            field.at[s, :, :, low_rows, :], halo.at[s, :, :, high_halo, :],
            ysend.at[1], yrecv.at[2 * s + 1], device_id=in_group(-1, 0), device_id_type=MESH,
        ).start()
    pass_on(0)

    load_pot.wait()
    load_table.wait()
    diagonal = 3.0 * half_weights[0] - center[0]

    def halves(value):
        total = value[0:8]
        for at in range(8, ry, 8):
            total = total + value[at : at + 8]
        return total

    def add_forms(sums, u, v):
        re = halves(u[0] * v[0] - u[1] * v[1])
        im = halves(u[0] * v[1] + u[1] * v[0])
        return (sums[0] + re, sums[1] + im)

    def rows_of(c, x):
        return pl.ds(pl.multiple_of((c * cx + x) * ry, ry), ry)

    def put_split(c, x, value):
        high = value.astype(jnp.bfloat16)
        split[rows_of(c, x), 0:LANES] = high
        split[rows_of(c, x), LANES : 2 * LANES] = (value - high.astype(jnp.float32)).astype(jnp.bfloat16)

    def multiply(matrix):
        zpart[...] = jnp.dot(split[...], matrix[...], preferred_element_type=jnp.float32)

    def stage(buf, s):
        def step(g, carry):
            for i in range(group):
                for c in range(2):
                    put_split(c, g * group + i, buf[s, c, g * group + i, own, :])
            return carry

        lax.fori_loop(0, cx // group, step, 0)

    def along_lanes(c, x):
        return zpart[rows_of(c, x), 0:LANES] + zpart[rows_of(c, x), LANES : 2 * LANES]

    def local_image(s, carry):
        stage(field, s)
        multiply(two_sided)

        def step(g, carry):
            for i in range(group):
                x = g * group + i
                scale = poten[x] + diagonal
                for c in range(2):
                    total = scale * field[s, c, x, own, :] + along_lanes(c, x)
                    for k in range(1, REACH + 1):
                        beside = field[s, c, (x + k) % cx, own, :] + field[s, c, (x + cx - k) % cx, own, :]
                        beside = beside + field[s, c, x, pl.ds(top - k, ry), :]
                        beside = beside + field[s, c, x, pl.ds(top + k, ry), :]
                        total = total + half_weights[k] * beside
                    image[s, c, x, own, :] = total
            return carry

        lax.fori_loop(0, cx // group, step, 0)
        return carry

    lax.fori_loop(0, nsrc, local_image, 0)
    hear(0)
    pass_on(1)

    wide = field.at[0, :, :, low_halo, :]
    narrow = field.at[0, :, first_half, low_halo, :]
    tile_zero = jnp.zeros((ry, LANES), jnp.float32)
    at_edge = (lane < REACH) | (lane >= LANES - REACH)

    def finish(s, carry):
        for i in range(2):
            pltpu.make_async_copy(wide, wide, yrecv.at[2 * s + i]).wait()
            pltpu.make_async_copy(left.at[s], left.at[s], zrecv.at[2 * s + i]).wait()
        edges = []
        belows = from_last(left[s])
        aboves = [jnp.where(low_part, 0.0, t) for t in (pltpu.roll(right[s], REACH, 1), right[s])]
        for below, above in zip(belows, aboves):
            total = tile_zero
            for k in range(1, REACH + 1):
                near = pltpu.roll(below, k, 1) * jnp.where(low_part, 0.0, half_weights[k])
                near = near + pltpu.roll(above, LANES - k, 1) * jnp.where(low_part, half_weights[k], 0.0)
                total = total + near
            edges.append(total)

        for x in range(cx):
            for c in range(2):
                f = image[s, c, x, own, :]
                moved = pltpu.roll(edges[c], (2 * LANES - REACH - 8 * x) % LANES, 1)
                down, up = zero, zero
                for k in range(1, REACH + 1):
                    down = down + half_weights[k] * halo[s, c, x, pl.ds(top - k, top), :]
                    up = up + half_weights[k] * halo[s, c, x, pl.ds(ry + k, top), :]
                image[s, c, x, own, :] = f + jnp.concatenate([down, up], 0) + jnp.where(at_edge, moved, 0.0)

        pltpu.make_async_remote_copy(
            image.at[s, :, first_half, high_rows, :], halo2.at[s, :, first_half, low_halo, :],
            y2send.at[0], y2recv.at[2 * s], device_id=in_group(1, 0), device_id_type=MESH,
        ).start()
        pltpu.make_async_remote_copy(
            image.at[s, :, second_half, low_rows, :], halo2.at[s, :, second_half, high_halo, :],
            y2send.at[1], y2recv.at[2 * s + 1], device_id=in_group(-1, 0), device_id_type=MESH,
        ).start()
        parts = strips_of(image, s)
        for c in range(2):
            image_strip[s, c] = parts[c]
        image_up[s] = last_lanes(parts)
        pltpu.make_async_remote_copy(
            image_up.at[s], left_image.at[s], z2send, z2recv.at[s],
            device_id=in_group(0, 1), device_id_type=MESH,
        ).start()
        return carry

    lax.fori_loop(0, nsrc, finish, 0)
    hear(1)
    pass_on(2)

    def inner(s, carry):
        stage(image, s)
        multiply(one_sided)
        sums = ((zero, zero),) * 4
        for upper in range(2):
            def pairs(g, sums):
                for i in range(group):
                    x = upper * half + g * group + i
                    scale = poten[x] + diagonal
                    b, w, once = [], [], []
                    for c in range(2):
                        f = image[s, c, x, own, :]
                        total = scale * f + along_lanes(c, x)
                        b.append(field[s, c, x, own, :])
                        for k in range(1, REACH + 1):
                            beside = image[s, c, (x + cx - k) % cx, own, :]
                            beside = beside + image[s, c, x, pl.ds(top + (k if upper else -k), ry), :]
                            total = total + 2.0 * half_weights[k] * beside
                        w.append(f)
                        once.append(total)
                    sides = ((b, b), (b, w), (w, w), (w, once))
                    sums = tuple(add_forms(old, *pair) for old, pair in zip(sums, sides))
                return sums

            sums = lax.fori_loop(0, half // group, pairs, sums)
        for i in range(4):
            for c in range(2):
                partial[2 * i + c, s] = sums[i][c]
        return carry

    lax.fori_loop(0, nsrc, inner, 0)

    spot = lax.broadcasted_iota(jnp.int32, (1, LANES), 1) // (LANES // (8 * nsrc))

    def gather_sums(quantities, row):
        for q in quantities:
            for s in range(nsrc):
                total = jnp.sum(partial[q, s], axis=0, keepdims=True)
                total = jnp.sum(total, axis=1, keepdims=True)
                row = jnp.where(spot == q * nsrc + s, total, row)
        return row

    row = gather_sums(range(6), jnp.zeros((1, LANES), jnp.float32))

    def across(s, carry):
        for i in range(2):
            pltpu.make_async_copy(narrow, narrow, y2recv.at[2 * s + i]).wait()
        pltpu.make_async_copy(left.at[s], left.at[s], z2recv.at[s]).wait()
        once = []
        for below in from_last(left_image[s]):
            total = tile_zero
            for k in range(1, REACH + 1):
                total = total + 2.0 * half_weights[k] * pltpu.roll(below, k, 1)
            once.append(jnp.where(low_part, 0.0, total))
        sums = add_forms((partial[6, s], partial[7, s]), (image_strip[s, 0], image_strip[s, 1]), once)
        for upper in range(2):
            def step(g, sums):
                for i in range(group):
                    x = upper * half + g * group + i
                    w, once = [], []
                    for c in range(2):
                        total = zero
                        for k in range(1, REACH + 1):
                            at = ry + k if upper else top - k
                            total = total + 2.0 * half_weights[k] * halo2[s, c, x, pl.ds(at, top), :]
                        once.append(total)
                        w.append(image[s, c, x, pl.ds(ry if upper else top, top), :])
                    re = w[0] * once[0] - w[1] * once[1]
                    im = w[0] * once[1] + w[1] * once[0]
                    sums = (sums[0] + re, sums[1] + im)
                return sums

            sums = lax.fori_loop(0, half // group, step, sums)
        for c in range(2):
            partial[6 + c, s] = sums[c]
        return carry

    lax.fori_loop(0, nsrc, across, 0)
    moments[...] = gather_sums(range(6, 8), row)
    hear(2)

    for j, (dy, dz) in enumerate(offsets):
        pltpu.make_async_remote_copy(
            moments, received.at[j], asend, arecv, device_id=in_group(dy, dz), device_id_type=MESH,
        ).start()
    pltpu.make_async_copy(received, received, arecv).wait()
    total = moments[...]
    for j in range(len(offsets)):
        total = total + received[j]

    wide_total = jnp.broadcast_to(total, (QPTS, LANES))
    lanes_each = LANES // 8
    forms = [
        wide_total if q == 0 else pltpu.roll(wide_total, LANES - q * lanes_each, 1) for q in range(8)
    ]
    reach = radius[0]
    shift = (reach * table[0], reach * table[1])
    parts = coefficients([(forms[2 * i], forms[2 * i + 1]) for i in range(4)], shift)
    weights = {}
    for k in range(MOMS):
        factor = (reach * table[2 + 2 * k], reach * table[3 + 2 * k])
        for i, part in enumerate(parts):
            both = complex_mul(factor, part)
            for c in range(2):
                weights[k, i, c] = jnp.sum(both[c], axis=0, keepdims=True)

    first = lax.axis_index("quad") * slab
    write_output(out, field, image, weights, first, slab, own, nsrc)

    for i, strip in enumerate((low_halo, high_halo)):
        every = field.at[:, :, :, strip, :]
        pltpu.make_async_copy(every, every, ysend.at[i]).wait()
        pltpu.make_async_copy(up, up, zsend.at[i]).wait()
        every = image.at[:, :, first_half, strip, :]
        pltpu.make_async_copy(every, every, y2send.at[i]).wait()
    pltpu.make_async_copy(image_up, image_up, z2send).wait()
    pltpu.make_async_copy(received, received, asend).wait()


def write_output(out, field, image, weights, first, slab, own, nsrc):
    for s in range(nsrc):
        lane_at = s * (LANES // (8 * nsrc))
        for k in range(MOMS):
            a = [weights[k, 0, c][:, lane_at : lane_at + 1] for c in range(2)]
            d = [weights[k, 1, c][:, lane_at : lane_at + 1] for c in range(2)]
            for x in range(slab):
                b = [field[s, c, first + x, own, :] for c in range(2)]
                w = [image[s, c, first + x, own, :] for c in range(2)]
                out[k, 0, s, x] = a[0] * b[0] - a[1] * b[1] + d[0] * w[0] - d[1] * w[1]
                out[k, 1, s, x] = a[0] * b[1] + a[1] * b[0] + d[0] * w[1] + d[1] * w[0]


def solution(mesh):
    nquad, ny, nz = mesh.shape["quad"], mesh.shape["py"], mesh.shape["pz"]

    def per_device(source_real, source_imag, potential, center, radius):
        nsrc, cx, ry, width = source_real.shape
        vmem, smem, hbm = pltpu.VMEM, pltpu.SMEM, pltpu.HBM
        padded = (nsrc, 2, cx, ry + 16, width)
        strips = (nsrc, ry, width)
        peers = ny * nz - 1
        dma = pltpu.SemaphoreType.DMA
        f32 = jnp.float32

        def in_hbm(value):
            return pltpu.with_memory_space_constraint(value, hbm)

        return pl.pallas_call(
            functools.partial(kernel, ny, nz, nquad),
            out_shape=jax.ShapeDtypeStruct((MOMS, 2, nsrc, cx // nquad, ry, width), f32),
            in_specs=[
                pl.BlockSpec(memory_space=hbm),
                pl.BlockSpec(memory_space=hbm),
                pl.BlockSpec(memory_space=hbm),
                pl.BlockSpec(memory_space=smem),
                pl.BlockSpec(memory_space=smem),
                pl.BlockSpec(memory_space=hbm),
            ],
            out_specs=pl.BlockSpec(memory_space=vmem),
            scratch_shapes=[
                vmem(padded, f32), vmem(padded, f32), vmem(padded, f32), vmem(padded, f32),
                vmem((cx, ry, width), f32), vmem((2 + 2 * MOMS, QPTS, width), f32),
                vmem(strips, f32), vmem(strips, f32), vmem(strips, f32), vmem(strips, f32),
                vmem((nsrc, 2, ry, width), f32), vmem(strips, f32), vmem(strips, f32),
                vmem((2 * cx * ry, 2 * width), jnp.bfloat16), vmem((2 * cx * ry, 2 * width), f32),
                vmem((2 * width, 2 * width), jnp.bfloat16), vmem((2 * width, 2 * width), jnp.bfloat16),
                vmem((8, nsrc, 8, width), f32), vmem((peers, 1, width), f32), vmem((1, width), f32),
                dma((2 * nsrc + 2,)), dma((2,)), dma((2 * nsrc,)), dma((2,)), dma((2 * nsrc,)),
                dma((2,)), dma((2 * nsrc,)), dma, dma((nsrc,)), dma, dma,
                pltpu.SemaphoreType.REGULAR((len(RELAY),)),
            ],
            compiler_params=pltpu.CompilerParams(
                collective_id=0, has_side_effects=True, vmem_limit_bytes=32 * 1024 * 1024
            ),
        )(
            in_hbm(source_real), in_hbm(source_imag), in_hbm(potential), center, radius,
            in_hbm(jnp.asarray(tables())),
        )

    in_specs = (P(None, None, "py", "pz"), P(None, None, "py", "pz"), P(None, "py", "pz"), P(), P())
    out_specs = P(None, None, None, "quad", "py", "pz")
    return jax.shard_map(
        per_device, mesh=mesh, in_specs=in_specs, out_specs=out_specs, check_vma=False
    )
```

```python
import functools
import math

import jax
import jax.numpy as jnp
import numpy as np
from jax import lax
from jax.experimental import pallas as pl
from jax.experimental.pallas import tpu as pltpu
from jax.sharding import PartitionSpec as P

QPTS = 8
MOMS = 4
MESH = pl.DeviceIdType.MESH
LANES = 128
REACH = 4
stencil_weights = (-205.0 / 72.0, 8.0 / 5.0, -1.0 / 5.0, 8.0 / 315.0, -1.0 / 560.0)
half_weights = tuple(-0.5 * w for w in stencil_weights)


def complex_mul(left, right):
    return (left[0] * right[0] - left[1] * right[1], left[0] * right[1] + left[1] * right[0])


def complex_div(left, right):
    norm_sq = right[0] * right[0] + right[1] * right[1]
    return (
        (left[0] * right[0] + left[1] * right[1]) / norm_sq,
        (left[1] * right[0] - left[0] * right[1]) / norm_sq,
    )


def complex_sub(left, right):
    return (left[0] - right[0], left[1] - right[1])


def recip(value):
    norm_sq = value[0] * value[0] + value[1] * value[1]
    return (value[0] / norm_sq, -value[1] / norm_sq)


def coefficients(totals, shift):
    mu0, mu1, mu2, mu3 = totals
    tau = complex_div(mu1, mu0)
    tau_mu1 = complex_mul(tau, mu1)
    nu2 = complex_sub(mu2, tau_mu1)
    tau_mu2 = complex_mul(tau, mu2)
    nu3 = complex_sub(complex_sub(mu3, tau_mu2), complex_mul(tau, complex_sub(mu2, tau_mu1)))
    ratio = complex_div(nu3, nu2)
    slope = complex_div(nu2, mu0)
    alpha_first = recip(complex_sub(shift, tau))
    gamma = complex_mul(alpha_first, slope)
    alpha_next = recip(complex_sub(complex_sub(shift, ratio), gamma))
    image_part = complex_mul(alpha_first, alpha_next)
    back = complex_mul(image_part, complex_sub(gamma, tau))
    return (alpha_first[0] + back[0], alpha_first[1] + back[1]), image_part


def tables():
    theta = 2.0 * math.pi * (np.arange(QPTS) + 0.5) / QPTS
    rows = [np.cos(theta), np.sin(theta)]
    for k in range(1, MOMS + 1):
        rows += [np.cos(k * theta) / QPTS, np.sin(k * theta) / QPTS]
    return np.broadcast_to(np.stack(rows)[:, :, None], (2 + 2 * MOMS, QPTS, LANES)).astype(np.float32)


BESIDE = ((1, 0), (-1, 0), (0, 1), (0, -1))
RELAY = (BESIDE, ((2, 0), (-2, 0), (0, 2)), ((4, 0),))


def group_offsets(ny, nz):
    every = [(a, b) for a in range(-ny // 2 + 1, ny // 2 + 1) for b in range(-nz // 2 + 1, nz // 2 + 1)]
    every = [o for o in every if o != (0, 0)]
    return sorted(every, key=lambda o: -(abs(o[0]) + 2 * abs(o[1])))


def band(shape):
    at = lax.broadcasted_iota(jnp.int32, shape, 0) % LANES
    to = lax.broadcasted_iota(jnp.int32, shape, 1)
    ahead = to % LANES - at
    value = jnp.zeros(shape, jnp.float32)
    for k in range(1, REACH + 1):
        value = jnp.where(jnp.abs(ahead) == k, half_weights[k], value)
    high = value.astype(jnp.bfloat16)
    low = (value - high.astype(jnp.float32)).astype(jnp.bfloat16)
    return jnp.where(to < LANES, high.astype(jnp.float32), low.astype(jnp.float32)).astype(jnp.bfloat16)


def kernel(
    ny, nz, nquad, sr, si, pot, center, radius, points, out,
    field, image, halo, halo2, poten, table, up, down, left, right, image_strip, image_up, left_image,
    split, zpart, two_sided, partial, received, moments,
    load_sem, ysend, yrecv, zsend, zrecv, y2send, y2recv, z2send, z2recv, asend, arecv, entered,
):
    nsrc, cx, ry, _ = sr.shape
    slab = cx // nquad
    half = cx // 2
    group = 4
    top = 8
    own = pl.ds(top, ry)
    low_halo, high_halo = pl.ds(top - REACH, REACH), pl.ds(top + ry, REACH)
    low_rows, high_rows = pl.ds(top, REACH), pl.ds(top + ry - REACH, REACH)
    quad, py, pz = lax.axis_index("quad"), lax.axis_index("py"), lax.axis_index("pz")

    def in_group(dy, dz):
        return (quad, (py + dy + ny) % ny, (pz + dz + nz) % nz)

    offsets = group_offsets(ny, nz)
    first_half, second_half = pl.ds(0, half), pl.ds(half, half)

    loads = []
    for s in range(nsrc):
        for c, ref in enumerate((sr, si)):
            copy = pltpu.make_async_copy(ref.at[s], field.at[s, c, :, own, :], load_sem.at[2 * s + c])
            copy.start()
            loads.append(copy)
    load_pot = pltpu.make_async_copy(pot, poten, load_sem.at[2 * nsrc])
    load_pot.start()
    load_table = pltpu.make_async_copy(points, table, load_sem.at[2 * nsrc + 1])
    load_table.start()

    barrier = pltpu.get_barrier_semaphore()
    for dy, dz in BESIDE:
        pl.semaphore_signal(barrier, inc=1, device_id=in_group(dy, dz), device_id_type=MESH)

    def pass_on(stage_at):
        for dy, dz in RELAY[stage_at]:
            pl.semaphore_signal(
                entered.at[stage_at], inc=1, device_id=in_group(dy, dz), device_id_type=MESH
            )

    def hear(stage_at):
        pl.semaphore_wait(entered.at[stage_at], len(RELAY[stage_at]))

    lane = lax.broadcasted_iota(jnp.int32, (ry, LANES), 1)
    zero_tile = jnp.zeros((top, LANES), jnp.float32)
    zero = jnp.zeros((8, LANES), jnp.float32)

    def clear(i, carry):
        s = i // cx
        x = i % cx
        for c in range(2):
            for buf in (field, image):
                buf[s, c, x, pl.ds(0, top), :] = zero_tile
                buf[s, c, x, pl.ds(top + ry, top), :] = zero_tile
            for buf in (halo, halo2):
                for at in range(0, ry, top):
                    buf[s, c, x, pl.ds(top + at, top), :] = zero_tile
        return carry

    lax.fori_loop(0, nsrc * cx, clear, 0, unroll=2)
    two_sided[...] = band(two_sided.shape)

    for copy in loads:
        copy.wait()
    low_part = lane % 8 < REACH

    def strips_of(buf, s):
        parts = []
        for c in range(2):
            total = jnp.zeros((ry, LANES), jnp.float32)
            for x in range(cx):
                moved = pltpu.roll(buf[s, c, x, own, :], 8 * x + REACH, 1)
                total = jnp.where(lane // 8 == x, moved, total)
            parts.append(total)
        return parts

    def last_lanes(parts):
        return jnp.where(low_part, parts[0], pltpu.roll(parts[1], REACH, 1))

    def from_last(both):
        return [jnp.where(low_part, t, 0.0) for t in (both, pltpu.roll(both, LANES - REACH, 1))]

    def pack(s, carry):
        parts = strips_of(field, s)
        up[s] = last_lanes(parts)
        down[s] = jnp.where(low_part, pltpu.roll(parts[0], LANES - REACH, 1), parts[1])
        return carry

    lax.fori_loop(0, nsrc, pack, 0)
    pl.semaphore_wait(barrier, len(BESIDE))

    for s in range(nsrc):
        pltpu.make_async_remote_copy(
            up.at[s], left.at[s], zsend.at[0], zrecv.at[2 * s],
            device_id=in_group(0, 1), device_id_type=MESH,
        ).start()
        pltpu.make_async_remote_copy(
            down.at[s], right.at[s], zsend.at[1], zrecv.at[2 * s + 1],
            device_id=in_group(0, -1), device_id_type=MESH,
        ).start()

    for s in range(nsrc):
        pltpu.make_async_remote_copy(
            field.at[s, :, :, high_rows, :], halo.at[s, :, :, low_halo, :],
            ysend.at[0], yrecv.at[2 * s], device_id=in_group(1, 0), device_id_type=MESH,
        ).start()
        pltpu.make_async_remote_copy(
            field.at[s, :, :, low_rows, :], halo.at[s, :, :, high_halo, :],
            ysend.at[1], yrecv.at[2 * s + 1], device_id=in_group(-1, 0), device_id_type=MESH,
        ).start()
    pass_on(0)

    load_pot.wait()
    load_table.wait()
    diagonal = 3.0 * half_weights[0] - center[0]

    def halves(value):
        total = value[0:8]
        for at in range(8, ry, 8):
            total = total + value[at : at + 8]
        return total

    def add_forms(sums, u, v):
        re = halves(u[0] * v[0] - u[1] * v[1])
        im = halves(u[0] * v[1] + u[1] * v[0])
        return (sums[0] + re, sums[1] + im)

    def rows_of(s, c, x):
        return pl.ds(pl.multiple_of(((s * 2 + c) * cx + x) * ry, ry), ry)

    def put_split(s, c, x, value):
        high = value.astype(jnp.bfloat16)
        split[rows_of(s, c, x), 0:LANES] = high
        split[rows_of(s, c, x), LANES : 2 * LANES] = (value - high.astype(jnp.float32)).astype(jnp.bfloat16)

    def multiply(matrix):
        zpart[...] = jnp.dot(split[...], matrix[...], preferred_element_type=jnp.float32)

    def stage(buf, s):
        def step(g, carry):
            for i in range(group):
                for c in range(2):
                    put_split(s, c, g * group + i, buf[s, c, g * group + i, own, :])
            return carry

        lax.fori_loop(0, cx // group, step, 0)

    def along_lanes(s, c, x):
        return zpart[rows_of(s, c, x), 0:LANES] + zpart[rows_of(s, c, x), LANES : 2 * LANES]

    def local_image(s, carry):
        def step(g, carry):
            layers = [
                [field[s, c, (g * group + (cx + d)) % cx, own, :] for d in range(-REACH, group + REACH)]
                for c in range(2)
            ]
            for i in range(group):
                x = g * group + i
                scale = poten[x] + diagonal
                for c in range(2):
                    total = scale * layers[c][i + REACH] + along_lanes(s, c, x)
                    for k in range(1, REACH + 1):
                        beside = layers[c][i + REACH + k] + layers[c][i + REACH - k]
                        beside = beside + field[s, c, x, pl.ds(top - k, ry), :]
                        beside = beside + field[s, c, x, pl.ds(top + k, ry), :]
                        total = total + half_weights[k] * beside
                    image[s, c, x, own, :] = total
            return carry

        lax.fori_loop(0, cx // group, step, 0)
        return carry

    def stage_field(s, carry):
        stage(field, s)
        return carry

    lax.fori_loop(0, nsrc, stage_field, 0)
    multiply(two_sided)
    lax.fori_loop(0, nsrc, local_image, 0)
    hear(0)
    pass_on(1)

    wide = field.at[0, :, :, low_halo, :]
    narrow = field.at[0, :, first_half, low_halo, :]
    tile_zero = jnp.zeros((ry, LANES), jnp.float32)
    at_edge = (lane < REACH) | (lane >= LANES - REACH)

    def finish(s, carry):
        for i in range(2):
            pltpu.make_async_copy(wide, wide, yrecv.at[2 * s + i]).wait()
            pltpu.make_async_copy(left.at[s], left.at[s], zrecv.at[2 * s + i]).wait()
        edges = []
        belows = from_last(left[s])
        aboves = [jnp.where(low_part, 0.0, t) for t in (pltpu.roll(right[s], REACH, 1), right[s])]
        for below, above in zip(belows, aboves):
            total = tile_zero
            for k in range(1, REACH + 1):
                near = pltpu.roll(below, k, 1) * jnp.where(low_part, 0.0, half_weights[k])
                near = near + pltpu.roll(above, LANES - k, 1) * jnp.where(low_part, half_weights[k], 0.0)
                total = total + near
            edges.append(total)

        for x in range(cx):
            for c in range(2):
                f = image[s, c, x, own, :]
                moved = pltpu.roll(edges[c], (2 * LANES - REACH - 8 * x) % LANES, 1)
                down, up = zero, zero
                for k in range(1, REACH + 1):
                    down = down + half_weights[k] * halo[s, c, x, pl.ds(top - k, top), :]
                    up = up + half_weights[k] * halo[s, c, x, pl.ds(ry + k, top), :]
                image[s, c, x, own, :] = f + jnp.concatenate([down, up], 0) + jnp.where(at_edge, moved, 0.0)

        pltpu.make_async_remote_copy(
            image.at[s, :, first_half, high_rows, :], halo2.at[s, :, first_half, low_halo, :],
            y2send.at[0], y2recv.at[2 * s], device_id=in_group(1, 0), device_id_type=MESH,
        ).start()
        pltpu.make_async_remote_copy(
            image.at[s, :, second_half, low_rows, :], halo2.at[s, :, second_half, high_halo, :],
            y2send.at[1], y2recv.at[2 * s + 1], device_id=in_group(-1, 0), device_id_type=MESH,
        ).start()
        parts = strips_of(image, s)
        for c in range(2):
            image_strip[s, c] = parts[c]
        image_up[s] = last_lanes(parts)
        pltpu.make_async_remote_copy(
            image_up.at[s], left_image.at[s], z2send, z2recv.at[s],
            device_id=in_group(0, 1), device_id_type=MESH,
        ).start()
        return carry

    lax.fori_loop(0, nsrc, finish, 0)
    hear(1)
    pass_on(2)

    inside = [jnp.where(lane >= k, 2.0 * half_weights[k], 0.0) for k in range(1, REACH + 1)]

    def inner(s, carry):
        sums = ((zero, zero),) * 4
        for upper in range(2):
            def pairs(g, sums):
                for i in range(group):
                    x = upper * half + g * group + i
                    scale = poten[x] + diagonal
                    b, w, once = [], [], []
                    for c in range(2):
                        f = image[s, c, x, own, :]
                        total = scale * f
                        b.append(field[s, c, x, own, :])
                        for k in range(1, REACH + 1):
                            beside = image[s, c, (x + cx - k) % cx, own, :]
                            beside = beside + image[s, c, x, pl.ds(top + (k if upper else -k), ry), :]
                            total = total + 2.0 * half_weights[k] * beside
                            total = total + inside[k - 1] * pltpu.roll(f, k, 1)
                        w.append(f)
                        once.append(total)
                    sides = ((b, b), (b, w), (w, w), (w, once))
                    sums = tuple(add_forms(old, *pair) for old, pair in zip(sums, sides))
                return sums

            sums = lax.fori_loop(0, half // group, pairs, sums)
        for i in range(4):
            for c in range(2):
                partial[2 * i + c, s] = sums[i][c]
        return carry

    lax.fori_loop(0, nsrc, inner, 0)

    spot = lax.broadcasted_iota(jnp.int32, (1, LANES), 1) // (LANES // (8 * nsrc))

    def gather_sums(quantities, row):
        for q in quantities:
            for s in range(nsrc):
                total = jnp.sum(partial[q, s], axis=0, keepdims=True)
                total = jnp.sum(total, axis=1, keepdims=True)
                row = jnp.where(spot == q * nsrc + s, total, row)
        return row

    row = gather_sums(range(6), jnp.zeros((1, LANES), jnp.float32))

    def across(s, carry):
        for i in range(2):
            pltpu.make_async_copy(narrow, narrow, y2recv.at[2 * s + i]).wait()
        pltpu.make_async_copy(left.at[s], left.at[s], z2recv.at[s]).wait()
        once = []
        for below in from_last(left_image[s]):
            total = tile_zero
            for k in range(1, REACH + 1):
                total = total + 2.0 * half_weights[k] * pltpu.roll(below, k, 1)
            once.append(jnp.where(low_part, 0.0, total))
        sums = add_forms((partial[6, s], partial[7, s]), (image_strip[s, 0], image_strip[s, 1]), once)
        found = [[sums], []]
        for x in range(cx):
            upper = x >= half
            w, once = [], []
            for c in range(2):
                total = zero
                for k in range(1, REACH + 1):
                    at = ry + k if upper else top - k
                    total = total + 2.0 * half_weights[k] * halo2[s, c, x, pl.ds(at, top), :]
                once.append(total)
                w.append(image[s, c, x, pl.ds(ry if upper else top, top), :])
            found[x % 2].append(complex_mul(w, once))
        totals = []
        for c in range(2):
            both = [sum((f[c] for f in side[1:]), side[0][c]) for side in found]
            totals.append(both[0] + both[1])
        sums = tuple(totals)
        for c in range(2):
            partial[6 + c, s] = sums[c]
        return carry

    lax.fori_loop(0, nsrc, across, 0)
    moments[...] = gather_sums(range(6, 8), row)
    hear(2)

    for j, (dy, dz) in enumerate(offsets):
        pltpu.make_async_remote_copy(
            moments, received.at[j], asend, arecv, device_id=in_group(dy, dz), device_id_type=MESH,
        ).start()
    pltpu.make_async_copy(received, received, arecv).wait()
    chains = [moments[...]] + [received[j] for j in range(3)]
    for j in range(3, len(offsets)):
        chains[j % 4] = chains[j % 4] + received[j]
    total = (chains[0] + chains[1]) + (chains[2] + chains[3])

    wide_total = jnp.broadcast_to(total, (QPTS, LANES))
    lanes_each = LANES // 8
    forms = [
        wide_total if q == 0 else pltpu.roll(wide_total, LANES - q * lanes_each, 1) for q in range(8)
    ]
    reach = radius[0]
    shift = (reach * table[0], reach * table[1])
    parts = coefficients([(forms[2 * i], forms[2 * i + 1]) for i in range(4)], shift)
    weights = {}
    for k in range(MOMS):
        factor = (reach * table[2 + 2 * k], reach * table[3 + 2 * k])
        for i, part in enumerate(parts):
            both = complex_mul(factor, part)
            for c in range(2):
                weights[k, i, c] = jnp.sum(both[c], axis=0, keepdims=True)

    first = lax.axis_index("quad") * slab
    write_output(out, field, image, weights, first, slab, own, nsrc)

    for i, strip in enumerate((low_halo, high_halo)):
        every = field.at[:, :, :, strip, :]
        pltpu.make_async_copy(every, every, ysend.at[i]).wait()
        pltpu.make_async_copy(up, up, zsend.at[i]).wait()
        every = image.at[:, :, first_half, strip, :]
        pltpu.make_async_copy(every, every, y2send.at[i]).wait()
    pltpu.make_async_copy(image_up, image_up, z2send).wait()
    pltpu.make_async_copy(received, received, asend).wait()


def write_output(out, field, image, weights, first, slab, own, nsrc):
    for s in range(nsrc):
        lane_at = s * (LANES // (8 * nsrc))
        for k in range(MOMS):
            a = [weights[k, 0, c][:, lane_at : lane_at + 1] for c in range(2)]
            d = [weights[k, 1, c][:, lane_at : lane_at + 1] for c in range(2)]
            for x in range(slab):
                b = [field[s, c, first + x, own, :] for c in range(2)]
                w = [image[s, c, first + x, own, :] for c in range(2)]
                out[k, 0, s, x] = a[0] * b[0] - a[1] * b[1] + d[0] * w[0] - d[1] * w[1]
                out[k, 1, s, x] = a[0] * b[1] + a[1] * b[0] + d[0] * w[1] + d[1] * w[0]


def solution(mesh):
    nquad, ny, nz = mesh.shape["quad"], mesh.shape["py"], mesh.shape["pz"]

    def per_device(source_real, source_imag, potential, center, radius):
        nsrc, cx, ry, width = source_real.shape
        vmem, smem, hbm = pltpu.VMEM, pltpu.SMEM, pltpu.HBM
        padded = (nsrc, 2, cx, ry + 16, width)
        strips = (nsrc, ry, width)
        peers = ny * nz - 1
        dma = pltpu.SemaphoreType.DMA
        f32 = jnp.float32

        def in_hbm(value):
            return pltpu.with_memory_space_constraint(value, hbm)

        return pl.pallas_call(
            functools.partial(kernel, ny, nz, nquad),
            out_shape=jax.ShapeDtypeStruct((MOMS, 2, nsrc, cx // nquad, ry, width), f32),
            in_specs=[
                pl.BlockSpec(memory_space=hbm),
                pl.BlockSpec(memory_space=hbm),
                pl.BlockSpec(memory_space=hbm),
                pl.BlockSpec(memory_space=smem),
                pl.BlockSpec(memory_space=smem),
                pl.BlockSpec(memory_space=hbm),
            ],
            out_specs=pl.BlockSpec(memory_space=vmem),
            scratch_shapes=[
                vmem(padded, f32), vmem(padded, f32), vmem(padded, f32), vmem(padded, f32),
                vmem((cx, ry, width), f32), vmem((2 + 2 * MOMS, QPTS, width), f32),
                vmem(strips, f32), vmem(strips, f32), vmem(strips, f32), vmem(strips, f32),
                vmem((nsrc, 2, ry, width), f32), vmem(strips, f32), vmem(strips, f32),
                vmem((2 * nsrc * cx * ry, 2 * width), jnp.bfloat16), vmem((2 * nsrc * cx * ry, 2 * width), f32),
                vmem((2 * width, 2 * width), jnp.bfloat16),
                vmem((8, nsrc, 8, width), f32), vmem((peers, 1, width), f32), vmem((1, width), f32),
                dma((2 * nsrc + 2,)), dma((2,)), dma((2 * nsrc,)), dma((2,)), dma((2 * nsrc,)),
                dma((2,)), dma((2 * nsrc,)), dma, dma((nsrc,)), dma, dma,
                pltpu.SemaphoreType.REGULAR((len(RELAY),)),
            ],
            compiler_params=pltpu.CompilerParams(
                collective_id=0, has_side_effects=True, vmem_limit_bytes=32 * 1024 * 1024
            ),
        )(
            in_hbm(source_real), in_hbm(source_imag), in_hbm(potential), center, radius,
            in_hbm(jnp.asarray(tables())),
        )

    in_specs = (P(None, None, "py", "pz"), P(None, None, "py", "pz"), P(None, "py", "pz"), P(), P())
    out_specs = P(None, None, None, "quad", "py", "pz")
    return jax.shard_map(
        per_device, mesh=mesh, in_specs=in_specs, out_specs=out_specs, check_vma=False
    )
```

```python
import functools
import math

import jax
import jax.numpy as jnp
import numpy as np
from jax import lax
from jax.experimental import pallas as pl
from jax.experimental.pallas import tpu as pltpu
from jax.sharding import PartitionSpec as P

QPTS = 8
MOMS = 4
MESH = pl.DeviceIdType.MESH
LANES = 128
REACH = 4
stencil_weights = (-205.0 / 72.0, 8.0 / 5.0, -1.0 / 5.0, 8.0 / 315.0, -1.0 / 560.0)
half_weights = tuple(-0.5 * w for w in stencil_weights)


def complex_mul(left, right):
    return (left[0] * right[0] - left[1] * right[1], left[0] * right[1] + left[1] * right[0])


def complex_div(left, right):
    norm_sq = right[0] * right[0] + right[1] * right[1]
    return (
        (left[0] * right[0] + left[1] * right[1]) / norm_sq,
        (left[1] * right[0] - left[0] * right[1]) / norm_sq,
    )


def complex_sub(left, right):
    return (left[0] - right[0], left[1] - right[1])


def recip(value):
    norm_sq = value[0] * value[0] + value[1] * value[1]
    return (value[0] / norm_sq, -value[1] / norm_sq)


def coefficients(totals, shift):
    mu0, mu1, mu2, mu3 = totals
    tau = complex_div(mu1, mu0)
    tau_mu1 = complex_mul(tau, mu1)
    nu2 = complex_sub(mu2, tau_mu1)
    tau_mu2 = complex_mul(tau, mu2)
    nu3 = complex_sub(complex_sub(mu3, tau_mu2), complex_mul(tau, complex_sub(mu2, tau_mu1)))
    ratio = complex_div(nu3, nu2)
    slope = complex_div(nu2, mu0)
    alpha_first = recip(complex_sub(shift, tau))
    gamma = complex_mul(alpha_first, slope)
    alpha_next = recip(complex_sub(complex_sub(shift, ratio), gamma))
    image_part = complex_mul(alpha_first, alpha_next)
    back = complex_mul(image_part, complex_sub(gamma, tau))
    return (alpha_first[0] + back[0], alpha_first[1] + back[1]), image_part


def tables():
    theta = 2.0 * math.pi * (np.arange(QPTS) + 0.5) / QPTS
    rows = [np.cos(theta), np.sin(theta)]
    for k in range(1, MOMS + 1):
        rows += [np.cos(k * theta) / QPTS, np.sin(k * theta) / QPTS]
    return np.broadcast_to(np.stack(rows)[:, :, None], (2 + 2 * MOMS, QPTS, LANES)).astype(np.float32)


BESIDE = ((1, 0), (-1, 0), (0, 1), (0, -1))
RELAY = (BESIDE, ((2, 0), (-2, 0), (0, 2)), ((4, 0),))


def group_offsets(ny, nz):
    every = [(a, b) for a in range(-ny // 2 + 1, ny // 2 + 1) for b in range(-nz // 2 + 1, nz // 2 + 1)]
    every = [o for o in every if o != (0, 0)]
    return sorted(every, key=lambda o: -(abs(o[0]) + 2 * abs(o[1])))


def band(shape):
    at = lax.broadcasted_iota(jnp.int32, shape, 0) % LANES
    to = lax.broadcasted_iota(jnp.int32, shape, 1)
    ahead = to % LANES - at
    value = jnp.zeros(shape, jnp.float32)
    for k in range(1, REACH + 1):
        value = jnp.where(jnp.abs(ahead) == k, half_weights[k], value)
    high = value.astype(jnp.bfloat16)
    low = (value - high.astype(jnp.float32)).astype(jnp.bfloat16)
    return jnp.where(to < LANES, high.astype(jnp.float32), low.astype(jnp.float32)).astype(jnp.bfloat16)


def kernel(
    ny, nz, nquad, sr, si, pot, center, radius, points, out,
    field, image, halo, halo2, poten, table, up, down, left, right, image_strip, image_up, left_image,
    split, zpart, two_sided, partial, received, moments,
    load_sem, ysend, yrecv, zsend, zrecv, y2send, y2recv, z2send, z2recv, asend, arecv, entered,
):
    nsrc, cx, ry, _ = sr.shape
    slab = cx // nquad
    half = cx // 2
    group = 4
    top = 8
    own = pl.ds(top, ry)
    low_halo, high_halo = pl.ds(top - REACH, REACH), pl.ds(top + ry, REACH)
    low_rows, high_rows = pl.ds(top, REACH), pl.ds(top + ry - REACH, REACH)
    quad, py, pz = lax.axis_index("quad"), lax.axis_index("py"), lax.axis_index("pz")

    def in_group(dy, dz):
        return (quad, (py + dy + ny) % ny, (pz + dz + nz) % nz)

    offsets = group_offsets(ny, nz)
    first_half, second_half = pl.ds(0, half), pl.ds(half, half)

    barrier = pltpu.get_barrier_semaphore()
    for dy, dz in BESIDE[::-1]:
        pl.semaphore_signal(barrier, inc=1, device_id=in_group(dy, dz), device_id_type=MESH)

    loads = []
    for s in range(nsrc):
        for c, ref in enumerate((sr, si)):
            copy = pltpu.make_async_copy(ref.at[s], field.at[s, c, :, own, :], load_sem.at[2 * s + c])
            copy.start()
            loads.append(copy)
    load_pot = pltpu.make_async_copy(pot, poten, load_sem.at[2 * nsrc])
    load_pot.start()
    load_table = pltpu.make_async_copy(points, table, load_sem.at[2 * nsrc + 1])
    load_table.start()

    def pass_on(stage_at):
        for dy, dz in RELAY[stage_at]:
            pl.semaphore_signal(
                entered.at[stage_at], inc=1, device_id=in_group(dy, dz), device_id_type=MESH
            )

    def hear(stage_at):
        pl.semaphore_wait(entered.at[stage_at], len(RELAY[stage_at]))

    lane = lax.broadcasted_iota(jnp.int32, (ry, LANES), 1)
    zero_tile = jnp.zeros((top, LANES), jnp.float32)
    zero = jnp.zeros((8, LANES), jnp.float32)

    def clear(i, carry):
        s = i // cx
        x = i % cx
        for c in range(2):
            for buf in (field, image):
                buf[s, c, x, pl.ds(0, top), :] = zero_tile
                buf[s, c, x, pl.ds(top + ry, top), :] = zero_tile
            for buf in (halo, halo2):
                for at in range(0, ry, top):
                    buf[s, c, x, pl.ds(top + at, top), :] = zero_tile
        return carry

    lax.fori_loop(0, nsrc * cx, clear, 0, unroll=2)
    two_sided[...] = band(two_sided.shape)

    low_part = lane % 8 < REACH

    def strips_of(buf, s):
        parts = []
        for c in range(2):
            total = jnp.zeros((ry, LANES), jnp.float32)
            for x in range(cx):
                moved = pltpu.roll(buf[s, c, x, own, :], 8 * x + REACH, 1)
                total = jnp.where(lane // 8 == x, moved, total)
            parts.append(total)
        return parts

    def last_lanes(parts):
        return jnp.where(low_part, parts[0], pltpu.roll(parts[1], REACH, 1))

    def from_last(both):
        return [jnp.where(low_part, t, 0.0) for t in (both, pltpu.roll(both, LANES - REACH, 1))]

    def pack(s, carry):
        parts = strips_of(field, s)
        up[s] = last_lanes(parts)
        down[s] = jnp.where(low_part, pltpu.roll(parts[0], LANES - REACH, 1), parts[1])
        return carry

    for s in range(nsrc):
        loads[2 * s].wait()
        loads[2 * s + 1].wait()
        pack(s, 0)
    pl.semaphore_wait(barrier, len(BESIDE))

    for s in range(nsrc):
        pltpu.make_async_remote_copy(
            field.at[s, :, :, high_rows, :], halo.at[s, :, :, low_halo, :],
            ysend.at[0], yrecv.at[2 * s], device_id=in_group(1, 0), device_id_type=MESH,
        ).start()
        pltpu.make_async_remote_copy(
            field.at[s, :, :, low_rows, :], halo.at[s, :, :, high_halo, :],
            ysend.at[1], yrecv.at[2 * s + 1], device_id=in_group(-1, 0), device_id_type=MESH,
        ).start()

    for s in range(nsrc):
        pltpu.make_async_remote_copy(
            up.at[s], left.at[s], zsend.at[0], zrecv.at[2 * s],
            device_id=in_group(0, 1), device_id_type=MESH,
        ).start()
        pltpu.make_async_remote_copy(
            down.at[s], right.at[s], zsend.at[1], zrecv.at[2 * s + 1],
            device_id=in_group(0, -1), device_id_type=MESH,
        ).start()
    pass_on(0)

    load_pot.wait()
    load_table.wait()
    diagonal = 3.0 * half_weights[0] - center[0]

    def halves(value):
        total = value[0:8]
        for at in range(8, ry, 8):
            total = total + value[at : at + 8]
        return total

    def add_forms(sums, u, v):
        re = halves(u[0] * v[0] - u[1] * v[1])
        im = halves(u[0] * v[1] + u[1] * v[0])
        return (sums[0] + re, sums[1] + im)

    def rows_of(s, c, x):
        return pl.ds(pl.multiple_of(((s * 2 + c) * cx + x) * ry, ry), ry)

    def put_split(s, c, x, value):
        high = value.astype(jnp.bfloat16)
        split[rows_of(s, c, x), 0:LANES] = high
        split[rows_of(s, c, x), LANES : 2 * LANES] = (value - high.astype(jnp.float32)).astype(jnp.bfloat16)

    def multiply(matrix):
        zpart[...] = jnp.dot(split[...], matrix[...], preferred_element_type=jnp.float32)

    def stage(buf, s):
        def step(g, carry):
            for i in range(group):
                for c in range(2):
                    put_split(s, c, g * group + i, buf[s, c, g * group + i, own, :])
            return carry

        lax.fori_loop(0, cx // group, step, 0)

    def along_lanes(s, c, x):
        return zpart[rows_of(s, c, x), 0:LANES] + zpart[rows_of(s, c, x), LANES : 2 * LANES]

    def local_image(s, carry):
        def step(g, sums):
            layers = [
                [field[s, c, (g * group + (cx + d)) % cx, own, :] for d in range(-REACH, group + REACH)]
                for c in range(2)
            ]
            for i in range(group):
                x = g * group + i
                scale = poten[x] + diagonal
                for c in range(2):
                    total = scale * layers[c][i + REACH] + along_lanes(s, c, x)
                    for k in range(1, REACH + 1):
                        beside = layers[c][i + REACH + k] + layers[c][i + REACH - k]
                        beside = beside + field[s, c, x, pl.ds(top - k, ry), :]
                        beside = beside + field[s, c, x, pl.ds(top + k, ry), :]
                        total = total + half_weights[k] * beside
                    image[s, c, x, own, :] = total
                b = [layers[c][i + REACH] for c in range(2)]
                sums = add_forms(sums, b, b)
            return sums

        sums = lax.fori_loop(0, cx // group, step, (zero, zero))
        for c in range(2):
            partial[c, s] = sums[c]
        return carry

    def stage_field(s, carry):
        stage(field, s)
        return carry

    lax.fori_loop(0, nsrc, stage_field, 0)
    multiply(two_sided)
    lax.fori_loop(0, nsrc, local_image, 0)
    hear(0)
    pass_on(1)

    wide = field.at[0, :, :, low_halo, :]
    narrow = field.at[0, :, first_half, low_halo, :]
    tile_zero = jnp.zeros((ry, LANES), jnp.float32)
    at_edge = (lane < REACH) | (lane >= LANES - REACH)

    def finish(s, carry):
        for i in range(2):
            pltpu.make_async_copy(wide, wide, yrecv.at[2 * s + i]).wait()
            pltpu.make_async_copy(left.at[s], left.at[s], zrecv.at[2 * s + i]).wait()
        edges = []
        belows = from_last(left[s])
        aboves = [jnp.where(low_part, 0.0, t) for t in (pltpu.roll(right[s], REACH, 1), right[s])]
        for below, above in zip(belows, aboves):
            total = tile_zero
            for k in range(1, REACH + 1):
                near = pltpu.roll(below, k, 1) * jnp.where(low_part, 0.0, half_weights[k])
                near = near + pltpu.roll(above, LANES - k, 1) * jnp.where(low_part, half_weights[k], 0.0)
                total = total + near
            edges.append(total)

        for x in range(cx):
            for c in range(2):
                f = image[s, c, x, own, :]
                moved = pltpu.roll(edges[c], (2 * LANES - REACH - 8 * x) % LANES, 1)
                down, up = zero, zero
                for k in range(1, REACH + 1):
                    down = down + half_weights[k] * halo[s, c, x, pl.ds(top - k, top), :]
                    up = up + half_weights[k] * halo[s, c, x, pl.ds(ry + k, top), :]
                image[s, c, x, own, :] = f + jnp.concatenate([down, up], 0) + jnp.where(at_edge, moved, 0.0)

        pltpu.make_async_remote_copy(
            image.at[s, :, first_half, high_rows, :], halo2.at[s, :, first_half, low_halo, :],
            y2send.at[0], y2recv.at[2 * s], device_id=in_group(1, 0), device_id_type=MESH,
        ).start()
        pltpu.make_async_remote_copy(
            image.at[s, :, second_half, low_rows, :], halo2.at[s, :, second_half, high_halo, :],
            y2send.at[1], y2recv.at[2 * s + 1], device_id=in_group(-1, 0), device_id_type=MESH,
        ).start()
        parts = strips_of(image, s)
        for c in range(2):
            image_strip[s, c] = parts[c]
        image_up[s] = last_lanes(parts)
        pltpu.make_async_remote_copy(
            image_up.at[s], left_image.at[s], z2send, z2recv.at[s],
            device_id=in_group(0, 1), device_id_type=MESH,
        ).start()
        return carry

    lax.fori_loop(0, nsrc, finish, 0)
    hear(1)
    pass_on(2)

    inside = [jnp.where(lane >= k, 2.0 * half_weights[k], 0.0) for k in range(1, REACH + 1)]

    def inner(s, carry):
        sums = ((zero, zero),) * 3
        for upper in range(2):
            def pairs(g, sums):
                for i in range(group):
                    x = upper * half + g * group + i
                    scale = poten[x] + diagonal
                    b, w, once = [], [], []
                    for c in range(2):
                        f = image[s, c, x, own, :]
                        total = scale * f
                        b.append(field[s, c, x, own, :])
                        for k in range(1, REACH + 1):
                            beside = image[s, c, (x + cx - k) % cx, own, :]
                            beside = beside + image[s, c, x, pl.ds(top + (k if upper else -k), ry), :]
                            total = total + 2.0 * half_weights[k] * beside
                            total = total + inside[k - 1] * pltpu.roll(f, k, 1)
                        w.append(f)
                        once.append(total)
                    sides = ((b, w), (w, w), (w, once))
                    sums = tuple(add_forms(old, *pair) for old, pair in zip(sums, sides))
                return sums

            sums = lax.fori_loop(0, half // group, pairs, sums)
        for i in range(3):
            for c in range(2):
                partial[2 * i + 2 + c, s] = sums[i][c]
        return carry

    lax.fori_loop(0, nsrc, inner, 0)

    spot = lax.broadcasted_iota(jnp.int32, (1, LANES), 1) // (LANES // (8 * nsrc))

    def gather_sums(quantities, row):
        for q in quantities:
            for s in range(nsrc):
                total = jnp.sum(partial[q, s], axis=0, keepdims=True)
                total = jnp.sum(total, axis=1, keepdims=True)
                row = jnp.where(spot == q * nsrc + s, total, row)
        return row

    row = gather_sums(range(6), jnp.zeros((1, LANES), jnp.float32))

    def across(s, carry):
        for i in range(2):
            pltpu.make_async_copy(narrow, narrow, y2recv.at[2 * s + i]).wait()
        pltpu.make_async_copy(left.at[s], left.at[s], z2recv.at[s]).wait()
        once = []
        for below in from_last(left_image[s]):
            total = tile_zero
            for k in range(1, REACH + 1):
                total = total + 2.0 * half_weights[k] * pltpu.roll(below, k, 1)
            once.append(jnp.where(low_part, 0.0, total))
        sums = add_forms((partial[6, s], partial[7, s]), (image_strip[s, 0], image_strip[s, 1]), once)
        found = [[sums], []]
        for x in range(cx):
            upper = x >= half
            w, once = [], []
            for c in range(2):
                total = zero
                for k in range(1, REACH + 1):
                    at = ry + k if upper else top - k
                    total = total + 2.0 * half_weights[k] * halo2[s, c, x, pl.ds(at, top), :]
                once.append(total)
                w.append(image[s, c, x, pl.ds(ry if upper else top, top), :])
            found[x % 2].append(complex_mul(w, once))
        totals = []
        for c in range(2):
            both = [sum((f[c] for f in side[1:]), side[0][c]) for side in found]
            totals.append(both[0] + both[1])
        sums = tuple(totals)
        for c in range(2):
            partial[6 + c, s] = sums[c]
        return carry

    lax.fori_loop(0, nsrc, across, 0)
    moments[...] = gather_sums(range(6, 8), row)
    hear(2)

    for j, (dy, dz) in enumerate(offsets):
        pltpu.make_async_remote_copy(
            moments, received.at[j], asend, arecv, device_id=in_group(dy, dz), device_id_type=MESH,
        ).start()
    pltpu.make_async_copy(received, received, arecv).wait()
    chains = [moments[...]] + [received[j] for j in range(3)]
    for j in range(3, len(offsets)):
        chains[j % 4] = chains[j % 4] + received[j]
    total = (chains[0] + chains[1]) + (chains[2] + chains[3])

    wide_total = jnp.broadcast_to(total, (QPTS, LANES))
    lanes_each = LANES // 8
    forms = [
        wide_total if q == 0 else pltpu.roll(wide_total, LANES - q * lanes_each, 1) for q in range(8)
    ]
    reach = radius[0]
    shift = (reach * table[0], reach * table[1])
    parts = coefficients([(forms[2 * i], forms[2 * i + 1]) for i in range(4)], shift)
    weights = {}
    for k in range(MOMS):
        factor = (reach * table[2 + 2 * k], reach * table[3 + 2 * k])
        for i, part in enumerate(parts):
            both = complex_mul(factor, part)
            for c in range(2):
                weights[k, i, c] = jnp.sum(both[c], axis=0, keepdims=True)

    first = lax.axis_index("quad") * slab
    write_output(out, field, image, weights, first, slab, own, nsrc)

    for i, strip in enumerate((low_halo, high_halo)):
        every = field.at[:, :, :, strip, :]
        pltpu.make_async_copy(every, every, ysend.at[i]).wait()
        pltpu.make_async_copy(up, up, zsend.at[i]).wait()
        every = image.at[:, :, first_half, strip, :]
        pltpu.make_async_copy(every, every, y2send.at[i]).wait()
    pltpu.make_async_copy(image_up, image_up, z2send).wait()
    pltpu.make_async_copy(received, received, asend).wait()


def write_output(out, field, image, weights, first, slab, own, nsrc):
    for s in range(nsrc):
        lane_at = s * (LANES // (8 * nsrc))
        for k in range(MOMS):
            a = [weights[k, 0, c][:, lane_at : lane_at + 1] for c in range(2)]
            d = [weights[k, 1, c][:, lane_at : lane_at + 1] for c in range(2)]
            for x in range(slab):
                b = [field[s, c, first + x, own, :] for c in range(2)]
                w = [image[s, c, first + x, own, :] for c in range(2)]
                out[k, 0, s, x] = a[0] * b[0] - a[1] * b[1] + d[0] * w[0] - d[1] * w[1]
                out[k, 1, s, x] = a[0] * b[1] + a[1] * b[0] + d[0] * w[1] + d[1] * w[0]


def solution(mesh):
    nquad, ny, nz = mesh.shape["quad"], mesh.shape["py"], mesh.shape["pz"]

    def per_device(source_real, source_imag, potential, center, radius):
        nsrc, cx, ry, width = source_real.shape
        vmem, smem, hbm = pltpu.VMEM, pltpu.SMEM, pltpu.HBM
        padded = (nsrc, 2, cx, ry + 16, width)
        strips = (nsrc, ry, width)
        peers = ny * nz - 1
        dma = pltpu.SemaphoreType.DMA
        f32 = jnp.float32

        def in_hbm(value):
            return pltpu.with_memory_space_constraint(value, hbm)

        return pl.pallas_call(
            functools.partial(kernel, ny, nz, nquad),
            out_shape=jax.ShapeDtypeStruct((MOMS, 2, nsrc, cx // nquad, ry, width), f32),
            in_specs=[
                pl.BlockSpec(memory_space=hbm),
                pl.BlockSpec(memory_space=hbm),
                pl.BlockSpec(memory_space=hbm),
                pl.BlockSpec(memory_space=smem),
                pl.BlockSpec(memory_space=smem),
                pl.BlockSpec(memory_space=hbm),
            ],
            out_specs=pl.BlockSpec(memory_space=vmem),
            scratch_shapes=[
                vmem(padded, f32), vmem(padded, f32), vmem(padded, f32), vmem(padded, f32),
                vmem((cx, ry, width), f32), vmem((2 + 2 * MOMS, QPTS, width), f32),
                vmem(strips, f32), vmem(strips, f32), vmem(strips, f32), vmem(strips, f32),
                vmem((nsrc, 2, ry, width), f32), vmem(strips, f32), vmem(strips, f32),
                vmem((2 * nsrc * cx * ry, 2 * width), jnp.bfloat16), vmem((2 * nsrc * cx * ry, 2 * width), f32),
                vmem((2 * width, 2 * width), jnp.bfloat16),
                vmem((8, nsrc, 8, width), f32), vmem((peers, 1, width), f32), vmem((1, width), f32),
                dma((2 * nsrc + 2,)), dma((2,)), dma((2 * nsrc,)), dma((2,)), dma((2 * nsrc,)),
                dma((2,)), dma((2 * nsrc,)), dma, dma((nsrc,)), dma, dma,
                pltpu.SemaphoreType.REGULAR((len(RELAY),)),
            ],
            compiler_params=pltpu.CompilerParams(
                collective_id=0, has_side_effects=True, vmem_limit_bytes=32 * 1024 * 1024
            ),
        )(
            in_hbm(source_real), in_hbm(source_imag), in_hbm(potential), center, radius,
            in_hbm(jnp.asarray(tables())),
        )

    in_specs = (P(None, None, "py", "pz"), P(None, None, "py", "pz"), P(None, "py", "pz"), P(), P())
    out_specs = P(None, None, None, "quad", "py", "pz")
    return jax.shard_map(
        per_device, mesh=mesh, in_specs=in_specs, out_specs=out_specs, check_vma=False
    )
```

```python
import functools
import math

import jax
import jax.numpy as jnp
import numpy as np
from jax import lax
from jax.experimental import pallas as pl
from jax.experimental.pallas import tpu as pltpu
from jax.sharding import PartitionSpec as P

QPTS = 8
MOMS = 4
MESH = pl.DeviceIdType.MESH
LANES = 128
REACH = 4
stencil_weights = (-205.0 / 72.0, 8.0 / 5.0, -1.0 / 5.0, 8.0 / 315.0, -1.0 / 560.0)
half_weights = tuple(-0.5 * w for w in stencil_weights)


def complex_mul(left, right):
    return (left[0] * right[0] - left[1] * right[1], left[0] * right[1] + left[1] * right[0])


def complex_div(left, right):
    norm_sq = right[0] * right[0] + right[1] * right[1]
    return (
        (left[0] * right[0] + left[1] * right[1]) / norm_sq,
        (left[1] * right[0] - left[0] * right[1]) / norm_sq,
    )


def complex_sub(left, right):
    return (left[0] - right[0], left[1] - right[1])


def recip(value):
    norm_sq = value[0] * value[0] + value[1] * value[1]
    return (value[0] / norm_sq, -value[1] / norm_sq)


def coefficients(totals, shift):
    mu0, mu1, mu2, mu3 = totals
    tau = complex_div(mu1, mu0)
    tau_mu1 = complex_mul(tau, mu1)
    nu2 = complex_sub(mu2, tau_mu1)
    tau_mu2 = complex_mul(tau, mu2)
    nu3 = complex_sub(complex_sub(mu3, tau_mu2), complex_mul(tau, complex_sub(mu2, tau_mu1)))
    ratio = complex_div(nu3, nu2)
    slope = complex_div(nu2, mu0)
    alpha_first = recip(complex_sub(shift, tau))
    gamma = complex_mul(alpha_first, slope)
    alpha_next = recip(complex_sub(complex_sub(shift, ratio), gamma))
    image_part = complex_mul(alpha_first, alpha_next)
    back = complex_mul(image_part, complex_sub(gamma, tau))
    return (alpha_first[0] + back[0], alpha_first[1] + back[1]), image_part


def tables():
    theta = 2.0 * math.pi * (np.arange(QPTS) + 0.5) / QPTS
    rows = [np.cos(theta), np.sin(theta)]
    for k in range(1, MOMS + 1):
        rows += [np.cos(k * theta) / QPTS, np.sin(k * theta) / QPTS]
    return np.broadcast_to(np.stack(rows)[:, :, None], (2 + 2 * MOMS, QPTS, LANES)).astype(np.float32)


BESIDE = ((1, 0), (-1, 0), (0, 1), (0, -1))
RELAY = (BESIDE, ((2, 0), (-2, 0), (0, 2)), ((4, 0),))


def group_offsets(ny, nz):
    every = [(a, b) for a in range(-ny // 2 + 1, ny // 2 + 1) for b in range(-nz // 2 + 1, nz // 2 + 1)]
    every = [o for o in every if o != (0, 0)]
    return sorted(every, key=lambda o: -(abs(o[0]) + 2 * abs(o[1])))


def band(shape):
    at = lax.broadcasted_iota(jnp.int32, shape, 0) % LANES
    to = lax.broadcasted_iota(jnp.int32, shape, 1)
    ahead = to % LANES - at
    value = jnp.zeros(shape, jnp.float32)
    for k in range(1, REACH + 1):
        value = jnp.where(jnp.abs(ahead) == k, half_weights[k], value)
    high = value.astype(jnp.bfloat16)
    low = (value - high.astype(jnp.float32)).astype(jnp.bfloat16)
    return jnp.where(to < LANES, high.astype(jnp.float32), low.astype(jnp.float32)).astype(jnp.bfloat16)


def kernel(
    ny, nz, nquad, sr, si, pot, center, radius, points, out,
    field, image, halo, halo2, poten, table, up, down, left, right, image_strip, image_up, left_image,
    split, zpart, two_sided, partial, received, moments,
    load_sem, ysend, yrecv, zsend, zrecv, y2send, y2recv, z2send, z2recv, asend, arecv, entered,
):
    nsrc, cx, ry, _ = sr.shape
    slab = cx // nquad
    half = cx // 2
    group = 8
    top = 8
    own = pl.ds(top, ry)
    low_halo, high_halo = pl.ds(top - REACH, REACH), pl.ds(top + ry, REACH)
    low_rows, high_rows = pl.ds(top, REACH), pl.ds(top + ry - REACH, REACH)
    quad, py, pz = lax.axis_index("quad"), lax.axis_index("py"), lax.axis_index("pz")

    def in_group(dy, dz):
        return (quad, (py + dy + ny) % ny, (pz + dz + nz) % nz)

    offsets = group_offsets(ny, nz)
    first_half, second_half = pl.ds(0, half), pl.ds(half, half)

    barrier = pltpu.get_barrier_semaphore()
    for dy, dz in BESIDE[::-1]:
        pl.semaphore_signal(barrier, inc=1, device_id=in_group(dy, dz), device_id_type=MESH)

    loads = []
    for s in range(nsrc):
        for c, ref in enumerate((sr, si)):
            copy = pltpu.make_async_copy(ref.at[s], field.at[s, c, :, own, :], load_sem.at[2 * s + c])
            copy.start()
            loads.append(copy)
    load_pot = pltpu.make_async_copy(pot, poten, load_sem.at[2 * nsrc])
    load_pot.start()
    load_table = pltpu.make_async_copy(points, table, load_sem.at[2 * nsrc + 1])
    load_table.start()

    def pass_on(stage_at):
        for dy, dz in RELAY[stage_at]:
            pl.semaphore_signal(
                entered.at[stage_at], inc=1, device_id=in_group(dy, dz), device_id_type=MESH
            )

    def hear(stage_at):
        pl.semaphore_wait(entered.at[stage_at], len(RELAY[stage_at]))

    lane = lax.broadcasted_iota(jnp.int32, (ry, LANES), 1)
    zero_tile = jnp.zeros((top, LANES), jnp.float32)
    zero = jnp.zeros((8, LANES), jnp.float32)

    def clear(i, carry):
        s = i // cx
        x = i % cx
        for c in range(2):
            for buf in (field, image):
                buf[s, c, x, pl.ds(0, top), :] = zero_tile
                buf[s, c, x, pl.ds(top + ry, top), :] = zero_tile
            for buf in (halo, halo2):
                for at in range(0, ry, top):
                    buf[s, c, x, pl.ds(top + at, top), :] = zero_tile
        return carry

    lax.fori_loop(0, nsrc * cx, clear, 0, unroll=2)
    two_sided[...] = band(two_sided.shape)

    low_part = lane % 8 < REACH

    def strips_of(buf, s):
        parts = []
        for c in range(2):
            total = jnp.zeros((ry, LANES), jnp.float32)
            for x in range(cx):
                moved = pltpu.roll(buf[s, c, x, own, :], 8 * x + REACH, 1)
                total = jnp.where(lane // 8 == x, moved, total)
            parts.append(total)
        return parts

    def last_lanes(parts):
        return jnp.where(low_part, parts[0], pltpu.roll(parts[1], REACH, 1))

    def from_last(both):
        return [jnp.where(low_part, t, 0.0) for t in (both, pltpu.roll(both, LANES - REACH, 1))]

    def pack(s, carry):
        parts = strips_of(field, s)
        up[s] = last_lanes(parts)
        down[s] = jnp.where(low_part, pltpu.roll(parts[0], LANES - REACH, 1), parts[1])
        return carry

    for s in range(nsrc):
        loads[2 * s].wait()
        loads[2 * s + 1].wait()
        pack(s, 0)
    pl.semaphore_wait(barrier, len(BESIDE))

    for s in range(nsrc):
        pltpu.make_async_remote_copy(
            field.at[s, :, :, high_rows, :], halo.at[s, :, :, low_halo, :],
            ysend.at[0], yrecv.at[2 * s], device_id=in_group(1, 0), device_id_type=MESH,
        ).start()
        pltpu.make_async_remote_copy(
            field.at[s, :, :, low_rows, :], halo.at[s, :, :, high_halo, :],
            ysend.at[1], yrecv.at[2 * s + 1], device_id=in_group(-1, 0), device_id_type=MESH,
        ).start()

    for s in range(nsrc):
        pltpu.make_async_remote_copy(
            up.at[s], left.at[s], zsend.at[0], zrecv.at[2 * s],
            device_id=in_group(0, 1), device_id_type=MESH,
        ).start()
        pltpu.make_async_remote_copy(
            down.at[s], right.at[s], zsend.at[1], zrecv.at[2 * s + 1],
            device_id=in_group(0, -1), device_id_type=MESH,
        ).start()
    pass_on(0)

    load_pot.wait()
    load_table.wait()
    diagonal = 3.0 * half_weights[0] - center[0]

    def halves(value):
        total = value[0:8]
        for at in range(8, ry, 8):
            total = total + value[at : at + 8]
        return total

    def add_forms(sums, u, v):
        re = halves(u[0] * v[0] - u[1] * v[1])
        im = halves(u[0] * v[1] + u[1] * v[0])
        return (sums[0] + re, sums[1] + im)

    def rows_of(s, c, x):
        return pl.ds(pl.multiple_of(((s * 2 + c) * cx + x) * ry, ry), ry)

    def put_split(s, c, x, value):
        high = value.astype(jnp.bfloat16)
        split[rows_of(s, c, x), 0:LANES] = high
        split[rows_of(s, c, x), LANES : 2 * LANES] = (value - high.astype(jnp.float32)).astype(jnp.bfloat16)

    def multiply(matrix):
        zpart[...] = jnp.dot(split[...], matrix[...], preferred_element_type=jnp.float32)

    def stage(buf, s):
        def step(g, carry):
            for i in range(group):
                for c in range(2):
                    put_split(s, c, g * group + i, buf[s, c, g * group + i, own, :])
            return carry

        lax.fori_loop(0, cx // group, step, 0)

    def along_lanes(s, c, x):
        return zpart[rows_of(s, c, x), 0:LANES] + zpart[rows_of(s, c, x), LANES : 2 * LANES]

    def local_image(s, carry):
        def step(g, sums):
            layers = [
                [field[s, c, (g * group + (cx + d)) % cx, own, :] for d in range(-REACH, group + REACH)]
                for c in range(2)
            ]
            for i in range(group):
                x = g * group + i
                scale = poten[x] + diagonal
                for c in range(2):
                    total = scale * layers[c][i + REACH] + along_lanes(s, c, x)
                    for k in range(1, REACH + 1):
                        beside = layers[c][i + REACH + k] + layers[c][i + REACH - k]
                        beside = beside + field[s, c, x, pl.ds(top - k, ry), :]
                        beside = beside + field[s, c, x, pl.ds(top + k, ry), :]
                        total = total + half_weights[k] * beside
                    image[s, c, x, own, :] = total
                b = [layers[c][i + REACH] for c in range(2)]
                sums = add_forms(sums, b, b)
            return sums

        sums = lax.fori_loop(0, cx // group, step, (zero, zero))
        for c in range(2):
            partial[c, s] = sums[c]
        return carry

    def stage_field(s, carry):
        stage(field, s)
        return carry

    lax.fori_loop(0, nsrc, stage_field, 0)
    multiply(two_sided)
    lax.fori_loop(0, nsrc, local_image, 0)
    hear(0)
    pass_on(1)

    wide = field.at[0, :, :, low_halo, :]
    narrow = field.at[0, :, first_half, low_halo, :]
    tile_zero = jnp.zeros((ry, LANES), jnp.float32)
    at_edge = (lane < REACH) | (lane >= LANES - REACH)

    def finish(s, carry):
        for i in range(2):
            pltpu.make_async_copy(wide, wide, yrecv.at[2 * s + i]).wait()
            pltpu.make_async_copy(left.at[s], left.at[s], zrecv.at[2 * s + i]).wait()
        edges = []
        belows = from_last(left[s])
        aboves = [jnp.where(low_part, 0.0, t) for t in (pltpu.roll(right[s], REACH, 1), right[s])]
        for below, above in zip(belows, aboves):
            total = tile_zero
            for k in range(1, REACH + 1):
                near = pltpu.roll(below, k, 1) * jnp.where(low_part, 0.0, half_weights[k])
                near = near + pltpu.roll(above, LANES - k, 1) * jnp.where(low_part, half_weights[k], 0.0)
                total = total + near
            edges.append(total)

        for x in range(cx):
            for c in range(2):
                f = image[s, c, x, own, :]
                moved = pltpu.roll(edges[c], (2 * LANES - REACH - 8 * x) % LANES, 1)
                down, up = zero, zero
                for k in range(1, REACH + 1):
                    down = down + half_weights[k] * halo[s, c, x, pl.ds(top - k, top), :]
                    up = up + half_weights[k] * halo[s, c, x, pl.ds(ry + k, top), :]
                image[s, c, x, own, :] = f + jnp.concatenate([down, up], 0) + jnp.where(at_edge, moved, 0.0)

        pltpu.make_async_remote_copy(
            image.at[s, :, first_half, high_rows, :], halo2.at[s, :, first_half, low_halo, :],
            y2send.at[0], y2recv.at[2 * s], device_id=in_group(1, 0), device_id_type=MESH,
        ).start()
        pltpu.make_async_remote_copy(
            image.at[s, :, second_half, low_rows, :], halo2.at[s, :, second_half, high_halo, :],
            y2send.at[1], y2recv.at[2 * s + 1], device_id=in_group(-1, 0), device_id_type=MESH,
        ).start()
        parts = strips_of(image, s)
        for c in range(2):
            image_strip[s, c] = parts[c]
        image_up[s] = last_lanes(parts)
        pltpu.make_async_remote_copy(
            image_up.at[s], left_image.at[s], z2send, z2recv.at[s],
            device_id=in_group(0, 1), device_id_type=MESH,
        ).start()
        return carry

    lax.fori_loop(0, nsrc, finish, 0)
    hear(1)
    pass_on(2)

    inside = [jnp.where(lane >= k, 2.0 * half_weights[k], 0.0) for k in range(1, REACH + 1)]

    def inner(s, carry):
        sums = ((zero, zero),) * 3
        for upper in range(2):
            def pairs(g, sums):
                for i in range(group):
                    x = upper * half + g * group + i
                    scale = poten[x] + diagonal
                    b, w, once = [], [], []
                    for c in range(2):
                        f = image[s, c, x, own, :]
                        total = scale * f
                        b.append(field[s, c, x, own, :])
                        for k in range(1, REACH + 1):
                            beside = image[s, c, (x + cx - k) % cx, own, :]
                            beside = beside + image[s, c, x, pl.ds(top + (k if upper else -k), ry), :]
                            total = total + 2.0 * half_weights[k] * beside
                            total = total + inside[k - 1] * pltpu.roll(f, k, 1)
                        w.append(f)
                        once.append(total)
                    sides = ((b, w), (w, w), (w, once))
                    sums = tuple(add_forms(old, *pair) for old, pair in zip(sums, sides))
                return sums

            sums = lax.fori_loop(0, half // group, pairs, sums)
        for i in range(3):
            for c in range(2):
                partial[2 * i + 2 + c, s] = sums[i][c]
        return carry

    lax.fori_loop(0, nsrc, inner, 0)

    spot = lax.broadcasted_iota(jnp.int32, (1, LANES), 1) // (LANES // (8 * nsrc))

    def gather_sums(quantities, row):
        for q in quantities:
            for s in range(nsrc):
                total = jnp.sum(partial[q, s], axis=0, keepdims=True)
                total = jnp.sum(total, axis=1, keepdims=True)
                row = jnp.where(spot == q * nsrc + s, total, row)
        return row

    row = gather_sums(range(6), jnp.zeros((1, LANES), jnp.float32))

    def across(s, carry):
        for i in range(2):
            pltpu.make_async_copy(narrow, narrow, y2recv.at[2 * s + i]).wait()
        pltpu.make_async_copy(left.at[s], left.at[s], z2recv.at[s]).wait()
        once = []
        for below in from_last(left_image[s]):
            total = tile_zero
            for k in range(1, REACH + 1):
                total = total + 2.0 * half_weights[k] * pltpu.roll(below, k, 1)
            once.append(jnp.where(low_part, 0.0, total))
        sums = add_forms((partial[6, s], partial[7, s]), (image_strip[s, 0], image_strip[s, 1]), once)
        found = [[sums], []]
        for x in range(cx):
            upper = x >= half
            w, once = [], []
            for c in range(2):
                total = zero
                for k in range(1, REACH + 1):
                    at = ry + k if upper else top - k
                    total = total + 2.0 * half_weights[k] * halo2[s, c, x, pl.ds(at, top), :]
                once.append(total)
                w.append(image[s, c, x, pl.ds(ry if upper else top, top), :])
            found[x % 2].append(complex_mul(w, once))
        totals = []
        for c in range(2):
            both = [sum((f[c] for f in side[1:]), side[0][c]) for side in found]
            totals.append(both[0] + both[1])
        sums = tuple(totals)
        for c in range(2):
            partial[6 + c, s] = sums[c]
        return carry

    lax.fori_loop(0, nsrc, across, 0)
    moments[...] = gather_sums(range(6, 8), row)
    hear(2)

    for j, (dy, dz) in enumerate(offsets):
        pltpu.make_async_remote_copy(
            moments, received.at[j], asend, arecv, device_id=in_group(dy, dz), device_id_type=MESH,
        ).start()
    pltpu.make_async_copy(received, received, arecv).wait()
    chains = [moments[...]] + [received[j] for j in range(3)]
    for j in range(3, len(offsets)):
        chains[j % 4] = chains[j % 4] + received[j]
    total = (chains[0] + chains[1]) + (chains[2] + chains[3])

    wide_total = jnp.broadcast_to(total, (QPTS, LANES))
    lanes_each = LANES // 8
    forms = [
        wide_total if q == 0 else pltpu.roll(wide_total, LANES - q * lanes_each, 1) for q in range(8)
    ]
    reach = radius[0]
    shift = (reach * table[0], reach * table[1])
    parts = coefficients([(forms[2 * i], forms[2 * i + 1]) for i in range(4)], shift)
    weights = {}
    for k in range(MOMS):
        factor = (reach * table[2 + 2 * k], reach * table[3 + 2 * k])
        for i, part in enumerate(parts):
            both = complex_mul(factor, part)
            for c in range(2):
                weights[k, i, c] = jnp.sum(both[c], axis=0, keepdims=True)

    first = lax.axis_index("quad") * slab
    write_output(out, field, image, weights, first, slab, own, nsrc)

    for i, strip in enumerate((low_halo, high_halo)):
        every = field.at[:, :, :, strip, :]
        pltpu.make_async_copy(every, every, ysend.at[i]).wait()
        pltpu.make_async_copy(up, up, zsend.at[i]).wait()
        every = image.at[:, :, first_half, strip, :]
        pltpu.make_async_copy(every, every, y2send.at[i]).wait()
    pltpu.make_async_copy(image_up, image_up, z2send).wait()
    pltpu.make_async_copy(received, received, asend).wait()


def write_output(out, field, image, weights, first, slab, own, nsrc):
    for s in range(nsrc):
        lane_at = s * (LANES // (8 * nsrc))
        for k in range(MOMS):
            a = [weights[k, 0, c][:, lane_at : lane_at + 1] for c in range(2)]
            d = [weights[k, 1, c][:, lane_at : lane_at + 1] for c in range(2)]
            for x in range(slab):
                b = [field[s, c, first + x, own, :] for c in range(2)]
                w = [image[s, c, first + x, own, :] for c in range(2)]
                out[k, 0, s, x] = a[0] * b[0] - a[1] * b[1] + d[0] * w[0] - d[1] * w[1]
                out[k, 1, s, x] = a[0] * b[1] + a[1] * b[0] + d[0] * w[1] + d[1] * w[0]


def solution(mesh):
    nquad, ny, nz = mesh.shape["quad"], mesh.shape["py"], mesh.shape["pz"]

    def per_device(source_real, source_imag, potential, center, radius):
        nsrc, cx, ry, width = source_real.shape
        vmem, smem, hbm = pltpu.VMEM, pltpu.SMEM, pltpu.HBM
        padded = (nsrc, 2, cx, ry + 16, width)
        strips = (nsrc, ry, width)
        peers = ny * nz - 1
        dma = pltpu.SemaphoreType.DMA
        f32 = jnp.float32

        def in_hbm(value):
            return pltpu.with_memory_space_constraint(value, hbm)

        return pl.pallas_call(
            functools.partial(kernel, ny, nz, nquad),
            out_shape=jax.ShapeDtypeStruct((MOMS, 2, nsrc, cx // nquad, ry, width), f32),
            in_specs=[
                pl.BlockSpec(memory_space=hbm),
                pl.BlockSpec(memory_space=hbm),
                pl.BlockSpec(memory_space=hbm),
                pl.BlockSpec(memory_space=smem),
                pl.BlockSpec(memory_space=smem),
                pl.BlockSpec(memory_space=hbm),
            ],
            out_specs=pl.BlockSpec(memory_space=vmem),
            scratch_shapes=[
                vmem(padded, f32), vmem(padded, f32), vmem(padded, f32), vmem(padded, f32),
                vmem((cx, ry, width), f32), vmem((2 + 2 * MOMS, QPTS, width), f32),
                vmem(strips, f32), vmem(strips, f32), vmem(strips, f32), vmem(strips, f32),
                vmem((nsrc, 2, ry, width), f32), vmem(strips, f32), vmem(strips, f32),
                vmem((2 * nsrc * cx * ry, 2 * width), jnp.bfloat16), vmem((2 * nsrc * cx * ry, 2 * width), f32),
                vmem((2 * width, 2 * width), jnp.bfloat16),
                vmem((8, nsrc, 8, width), f32), vmem((peers, 1, width), f32), vmem((1, width), f32),
                dma((2 * nsrc + 2,)), dma((2,)), dma((2 * nsrc,)), dma((2,)), dma((2 * nsrc,)),
                dma((2,)), dma((2 * nsrc,)), dma, dma((nsrc,)), dma, dma,
                pltpu.SemaphoreType.REGULAR((len(RELAY),)),
            ],
            compiler_params=pltpu.CompilerParams(
                collective_id=0, has_side_effects=True, vmem_limit_bytes=32 * 1024 * 1024
            ),
        )(
            in_hbm(source_real), in_hbm(source_imag), in_hbm(potential), center, radius,
            in_hbm(jnp.asarray(tables())),
        )

    in_specs = (P(None, None, "py", "pz"), P(None, None, "py", "pz"), P(None, "py", "pz"), P(), P())
    out_specs = P(None, None, None, "quad", "py", "pz")
    return jax.shard_map(
        per_device, mesh=mesh, in_specs=in_specs, out_specs=out_specs, check_vma=False
    )
```
